256 devices in a mesh: wide: 64 (over x, y, z_lo, core), pol: 4 (over z_hi).
Axes of the slice: x: 4, y: 4, z: 8 (z_hi: 4, z_lo: 2; z = z_hi * 2 + z_lo), core: 2. Of those that a mesh axis runs over, the one named last changes fastest.
Arguments:
- voltages: bfloat16 [2, 4, 1024, 128, 256], P(None, 'pol', 'wide'), may hold values from -6 to 6
- gains: float32 [2, 2, 1024, 128], P(None, None, 'wide'), may hold values from -0.04 to 0.04
- cylinder_feed_lookup: int32 [1024], replicated, may hold values from 0 to 1023, each once
- beam_bins: int32 [128, 256], P('wide'), may hold values from 0 to 511
Outputs:
- intensity: float32 [1024, 128, 256], P(('wide', 'pol'))
The draws below stay inside these ranges and needn't reach their ends.
Inputs may be any that keep to these rules, and one draw needn't show every extreme that they name: `cylinder_feed_lookup`: every feed of 0 to 1023 appears once.
All inputs are finite; a program needn't handle non-finite values.
Results may differ from the reference program's by a relative error of at most 0.0024.
Values may be sent and summed in bfloat16 or wider, within the bound.
No kernel may reach another device: no remote copies, remote signals or barrier semaphores. Data moves between devices by JAX's collectives and lax.ppermute only.
A program may use at most 64 MiB of HBM per device.

```python
import math
import jax
import jax.numpy as jnp
import numpy as np
from jax import lax

NSF = 256
CYL = 4
VOLTAGE_STREAMS = 4
WINDOW_SAMPLES = 256
FEED_SLOTS = 1024
BEAMS = 1024
FREQUENCY_BINS = 128


def place_ends(result, stream_key, low, high):
    place = [jax.random.randint(jax.random.fold_in(stream_key, axis), (), 0, length) for axis, length in enumerate(result.shape)]
    longest = result.shape.index(max(result.shape))
    next_to = place[:longest] + [(place[longest] + 1) % result.shape[longest]] + place[longest + 1:]
    return result.at[tuple(place)].set(low).at[tuple(next_to)].set(high)


def steps_of(key, dims, pieces, least, high):
    def one(axis_at, parts):
        draws = jax.random.uniform(jax.random.fold_in(jax.random.fold_in(key, 6), axis_at), (parts,), jnp.float32, least / len(pieces), high / len(pieces))
        return jnp.repeat(jnp.exp(draws), dims[axis_at] // parts).reshape((-1,) + (1,) * (len(dims) - axis_at - 1))

    factor_of = one(*pieces[0])
    for cut in pieces[1:]:
        factor_of = factor_of * one(*cut)
    return factor_of


def scatter_about(rng, shape, scale, limit, shards=(), kind=jnp.bfloat16):
    result = jax.random.normal(rng, shape, jnp.float32) * scale
    if len(shards) > 0:
        result = steps_of(rng, shape, shards, -0.22, 0.18) * result
    return jnp.clip(result, min=-limit, max=limit).astype(kind)


def setup_inputs(seed: int = 0) -> dict:
    keys = jax.random.split(jax.random.key(seed), 5)
    voltages = scatter_about(keys[0], (2, VOLTAGE_STREAMS, FEED_SLOTS, FREQUENCY_BINS, WINDOW_SAMPLES), 1.0, 6.0, ((1, 4), (2, 64)))
    gains = scatter_about(keys[1], (2, 2, FEED_SLOTS, FREQUENCY_BINS), 0.0078, 0.04, ((2, 64),), jnp.float32)
    cylinder_feed_lookup = jax.random.permutation(keys[2], FEED_SLOTS).astype(jnp.int32)
    beam_bins = place_ends(jax.random.randint(keys[3], (FREQUENCY_BINS, NSF), 0, 2 * NSF), jax.random.fold_in(keys[3], 1), 0, (2 * NSF) - 1).astype(jnp.int32)
    return {"voltages": voltages, "gains": gains, "cylinder_feed_lookup": cylinder_feed_lookup, "beam_bins": beam_bins}


def dft_table(bins, feeds_per):
    along = lax.iota(jnp.int32, feeds_per)
    product = (bins[:, :, None] * along[None, None, :]) % (2 * feeds_per)
    theta = product.astype(jnp.float32) * (math.pi / feeds_per)
    cos_table = jnp.cos(theta).astype(jnp.bfloat16)
    sin_table = jnp.sin(theta).astype(jnp.bfloat16)
    first = jnp.stack([cos_table, sin_table], axis=2)
    second = jnp.stack([-sin_table, cos_table], axis=2)
    return jnp.stack([first, second], axis=1)


def eastwest_beam_power(real_part, imag_part):
    steps = np.outer(np.arange(4), np.arange(4)) % 4
    cosine = jnp.asarray(np.array([1.0, 0.0, -1.0, 0.0])[steps], jnp.float32)
    sine = jnp.asarray(np.array([0.0, -1.0, 0.0, 1.0])[steps], jnp.float32)
    high = lax.Precision.HIGHEST
    beam_real_part = jnp.einsum('ec,...cbt->...ebt', cosine, real_part, precision=high) - jnp.einsum('ec,...cbt->...ebt', sine, imag_part, precision=high)
    beam_imag = jnp.einsum('ec,...cbt->...ebt', cosine, imag_part, precision=high) + jnp.einsum('ec,...cbt->...ebt', sine, real_part, precision=high)
    return beam_real_part * beam_real_part + beam_imag * beam_imag


def reference(voltages, gains, cylinder_feed_lookup, beam_bins):
    def channel(index):
        volts = lax.dynamic_index_in_dim(voltages, index, 3, keepdims=False).astype(jnp.float32)
        gain_now = lax.dynamic_index_in_dim(gains, index, 3, keepdims=False)
        gain_now = jnp.repeat(gain_now, 2, axis=1)
        gain_real = gain_now[0][:, :, None]
        gain_imag = gain_now[1][:, :, None]
        cal_real = gain_real * volts[0] - gain_imag * volts[1]
        cal_imag = gain_real * volts[1] + gain_imag * volts[0]
        calibrated = jnp.stack([cal_real, cal_imag]).astype(jnp.bfloat16)
        placed = jnp.take(calibrated, cylinder_feed_lookup, axis=2)
        grid = placed.reshape(2, VOLTAGE_STREAMS, CYL, NSF, WINDOW_SAMPLES)
        bins_now = lax.dynamic_index_in_dim(beam_bins, index, 0, keepdims=True)
        table = dft_table(bins_now, NSF)[0]
        fields = jnp.einsum('obin,iscnt->oscbt', table.astype(jnp.float32), grid.astype(jnp.float32), precision=lax.Precision.HIGHEST)
        power = eastwest_beam_power(fields[0], fields[1])
        return jnp.sum(power, axis=0).reshape(BEAMS, WINDOW_SAMPLES)

    stacked = lax.map(channel, jnp.arange(FREQUENCY_BINS, dtype=jnp.int32))
    return jnp.transpose(stacked, (1, 0, 2))
```

```python
import math

import jax
import jax.numpy as jnp
from jax import lax
from jax.experimental import pallas as pl
from jax.experimental.pallas import tpu as pltpu
from jax.sharding import PartitionSpec as P

HIGH = 100 * 2**20


def dft_table(bins, feeds_per):
    along = lax.iota(jnp.int32, feeds_per)
    product = bins[:, :, None] * along[None, None, :] % (2 * feeds_per)
    theta = product.astype(jnp.float32) * (math.pi / feeds_per)
    cos_table = jnp.cos(theta).astype(jnp.bfloat16)
    sin_table = jnp.sin(theta).astype(jnp.bfloat16)
    first = jnp.concatenate([cos_table, sin_table], axis=2)
    second = jnp.concatenate([-sin_table, cos_table], axis=2)
    return jnp.concatenate([first, second], axis=1)


def calibrate_kernel(volts_ref, gains_ref, out_ref, real_ref, imag_ref):
    feeds, block, samples = volts_ref.shape[2:]
    for half in range(samples // 128):
        lanes = pl.ds(half * 128, 128)
        real_ref[half] = volts_ref[0, 0, :, :, lanes].astype(jnp.float32).reshape(feeds * block, 128)
        imag_ref[half] = volts_ref[1, 0, :, :, lanes].astype(jnp.float32).reshape(feeds * block, 128)
    polar = lax.axis_index("pol") // 2
    gain_real = gains_ref[0, polar]
    gain_imag = gains_ref[1, polar]
    for channel in range(block):
        rows = pl.ds(channel, feeds, stride=block)
        for half in range(samples // 128):
            lanes = pl.ds(half * 128, 128)
            volt_real = real_ref[half, rows]
            volt_imag = imag_ref[half, rows]
            own_real = gain_real[:, channel : channel + 1]
            own_imag = gain_imag[:, channel : channel + 1]
            cal_real = own_real * volt_real - own_imag * volt_imag
            cal_imag = own_real * volt_imag + own_imag * volt_real
            out_ref[channel // 2, channel % 2, 0, :, lanes] = cal_real.astype(jnp.bfloat16)
            out_ref[channel // 2, channel % 2, 1, :, lanes] = cal_imag.astype(jnp.bfloat16)


def calibrate(voltages, gains):
    _, _, feeds, channels, samples = voltages.shape
    block = 128
    return pl.pallas_call(
        calibrate_kernel,
        out_shape=jax.ShapeDtypeStruct((channels // 2, 2, 2, feeds, samples), jnp.bfloat16),
        grid=(channels // block,),
        in_specs=[
            pl.BlockSpec((2, 1, feeds, block, samples), lambda i: (0, 0, 0, i, 0)),
            pl.BlockSpec((2, 2, feeds, block), lambda i: (0, 0, 0, i)),
        ],
        out_specs=pl.BlockSpec((block // 2, 2, 2, feeds, samples), lambda i: (i, 0, 0, 0, 0)),
        scratch_shapes=[pltpu.VMEM((samples // 128, feeds * block, 128), jnp.float32)] * 2,
        compiler_params=pltpu.CompilerParams(vmem_limit_bytes=40 * 2**20),
        cost_estimate=pl.CostEstimate(flops=8 * 2**20, bytes_accessed=4 * 2**20, transcendentals=0),
        name="calibrate",
    )(voltages, gains)


def beams_kernel(turned_ref, place_ref, table_ref, out_ref, field_ref):
    step = pl.program_id(0)
    sources, channels, _, feeds, samples = turned_ref.shape
    feeds_total = sources * feeds
    for channel in range(channels):
        parts = []
        for part in range(2):
            own = turned_ref[:, channel, part].reshape(feeds_total, samples)
            placed = jnp.dot(place_ref[...], own, preferred_element_type=jnp.float32)
            parts.append(placed.astype(jnp.bfloat16))
        grid = jnp.concatenate(parts, axis=0)
        field_ref[step, channel] = jnp.dot(table_ref[channel], grid, preferred_element_type=jnp.float32)

    @pl.when(step == pl.num_programs(0) - 1)
    def _():
        beams = field_ref.shape[2] // 2
        for row in range(0, beams, 8):
            for half in range(samples // 128):
                lanes = pl.ds(half * 128, 128)
                powers = []
                for channel in range(channels):
                    re = [field_ref[c, channel, pl.ds(row, 8), lanes] for c in range(4)]
                    im = [field_ref[c, channel, pl.ds(beams + row, 8), lanes] for c in range(4)]
                    sum_re, sum_im = re[0] + re[2], im[0] + im[2]
                    dif_re, dif_im = re[0] - re[2], im[0] - im[2]
                    odd_re, odd_im = re[1] + re[3], im[1] + im[3]
                    odd_dif_re, odd_dif_im = re[1] - re[3], im[1] - im[3]
                    each = [
                        (sum_re + odd_re, sum_im + odd_im),
                        (dif_re + odd_dif_im, dif_im - odd_dif_re),
                        (sum_re - odd_re, sum_im - odd_im),
                        (dif_re - odd_dif_im, dif_im + odd_dif_re),
                    ]
                    powers.append([a * a + b * b for a, b in each])
                for e in range(4):
                    low = jnp.concatenate([powers[0][e][:4], powers[1][e][:4]], axis=0)
                    high = jnp.concatenate([powers[0][e][4:], powers[1][e][4:]], axis=0)
                    at = e * (beams // 4) + row // 4
                    out_ref[at, pl.ds(half * 8, 8)] = low.astype(jnp.bfloat16)
                    out_ref[at + 1, pl.ds(half * 8, 8)] = high.astype(jnp.bfloat16)


def form_beams(turned, place, table):
    sources, channels, _, feeds, samples = turned.shape
    feeds_total = sources * feeds
    return pl.pallas_call(
        beams_kernel,
        out_shape=jax.ShapeDtypeStruct((feeds_total // 4, 16, 128), jnp.bfloat16),
        grid=(4,),
        in_specs=[
            pl.BlockSpec(turned.shape, lambda i: (0, 0, 0, 0, 0)),
            pl.BlockSpec((feeds_total // 4, feeds_total), lambda i: (i, 0)),
            pl.BlockSpec(table.shape, lambda i: (0, 0, 0)),
        ],
        out_specs=pl.BlockSpec((feeds_total // 4, 16, 128), lambda i: (0, 0, 0)),
        scratch_shapes=[pltpu.VMEM((4, channels, feeds_total // 2, samples), jnp.float32)],
        compiler_params=pltpu.CompilerParams(vmem_limit_bytes=40 * 2**20),
        cost_estimate=pl.CostEstimate(flops=3 * 2**30, bytes_accessed=6 * 2**20, transcendentals=0),
        name="form_beams",
    )(turned, place, table)


def total_kernel(sent_ref, out_ref, total_ref):
    block = sent_ref.shape[0]
    total = sent_ref[:, 0].astype(jnp.float32)
    for stream in range(1, 4):
        total += sent_ref[:, stream].astype(jnp.float32)
    for half in range(2):
        total_ref[half] = total[:, half * 8 : half * 8 + 8].reshape(block * 8, 128)
    for beam in range(4):
        for half in range(2):
            rows = total_ref[half, pl.ds(beam, 2 * block, stride=4)]
            out_ref[beam, :, pl.ds(half * 128, 128)] = rows


def add_streams(sent):
    blocks = sent.shape[0]
    block = 16
    return pl.pallas_call(
        total_kernel,
        out_shape=jax.ShapeDtypeStruct((4, 2 * blocks, 256), jnp.float32),
        grid=(blocks // block,),
        in_specs=[pl.BlockSpec((block, 4, 16, 128), lambda i: (i, 0, 0, 0))],
        out_specs=pl.BlockSpec((4, 2 * block, 256), lambda i: (0, i, 0)),
        scratch_shapes=[pltpu.VMEM((2, block * 8, 128), jnp.float32)],
        compiler_params=pltpu.CompilerParams(vmem_limit_bytes=16 * 2**20),
        cost_estimate=pl.CostEstimate(flops=2**20, bytes_accessed=2 * 2**20, transcendentals=0),
        name="add_streams",
    )(sent)


def body(voltages, gains, cylinder_feed_lookup, beam_bins):
    calibrated = calibrate(voltages, gains)
    turned = lax.all_to_all(calibrated, "wide", split_axis=0, concat_axis=0, tiled=True)
    feeds_total = cylinder_feed_lookup.shape[0]
    slots = lax.iota(jnp.int32, feeds_total)
    place = (cylinder_feed_lookup[:, None] == slots[None, :]).astype(jnp.bfloat16)
    table = dft_table(beam_bins, beam_bins.shape[1])
    power = form_beams(turned, place, table)
    sent = lax.all_to_all(power, ("wide", "pol"), split_axis=0, concat_axis=0, tiled=True)
    return add_streams(sent.reshape(-1, 4, 16, 128))


def solution(mesh):
    return jax.shard_map(
        body,
        mesh=mesh,
        in_specs=(
            P(None, "pol", "wide", None, None),
            P(None, None, "wide", None),
            P(),
            P("wide", None),
        ),
        out_specs=P(("wide", "pol"), None, None),
        check_vma=False,
    )
```

```python
import math

import jax
import jax.numpy as jnp
from jax import lax
from jax.experimental import pallas as pl
from jax.experimental.pallas import tpu as pltpu
from jax.sharding import PartitionSpec as P

MEGA = 2**20


def dft_table(bins, feeds_per):
    along = lax.iota(jnp.int32, feeds_per)
    product = bins[:, :, None] * along[None, None, :] % (2 * feeds_per)
    theta = product.astype(jnp.float32) * (math.pi / feeds_per)
    cos_table = jnp.cos(theta).astype(jnp.bfloat16)
    sin_table = jnp.sin(theta).astype(jnp.bfloat16)
    first = jnp.concatenate([cos_table, sin_table], axis=2)
    second = jnp.concatenate([-sin_table, cos_table], axis=2)
    return jnp.concatenate([first, second], axis=1)


def calibrate_kernel(volts_ref, gains_ref, out_ref, in_buf, out_buf, in_sem, out_sem):
    chunks, _, feeds, block, samples = in_buf.shape

    def fetch(i):
        own = volts_ref.at[:, 0, :, pl.ds(i * block, block), :]
        return pltpu.make_async_copy(own, in_buf.at[i], in_sem.at[i])

    def store(i):
        own = out_ref.at[pl.ds(i * block // 2, block // 2)]
        return pltpu.make_async_copy(out_buf.at[i], own, out_sem.at[i])

    for i in range(chunks):
        fetch(i).start()
    polar = lax.axis_index("pol") // 2
    gain_real = gains_ref[0, polar]
    gain_imag = gains_ref[1, polar]
    row = lax.broadcasted_iota(jnp.int32, (feeds * 16, feeds * 16), 0)
    col = lax.broadcasted_iota(jnp.int32, (feeds * 16, feeds * 16), 1)
    swap = (row // feeds == col % 16) & (row % feeds == col // 16)
    swap = swap.astype(jnp.float32).astype(jnp.bfloat16)
    for i in range(chunks):
        fetch(i).wait()
        for group in range(block // 16):
            parts = []
            for part in range(2):
                own = in_buf[i, part, :, group * 16 : group * 16 + 16, :].reshape(feeds * 16, samples)
                parts.append(jnp.dot(swap, own, preferred_element_type=jnp.float32))
            for c in range(16):
                at = group * 16 + c
                channel = i * block + at
                own_real = gain_real[:, channel : channel + 1]
                own_imag = gain_imag[:, channel : channel + 1]
                volt_real = parts[0][c * feeds : c * feeds + feeds]
                volt_imag = parts[1][c * feeds : c * feeds + feeds]
                cal_real = own_real * volt_real - own_imag * volt_imag
                cal_imag = own_real * volt_imag + own_imag * volt_real
                out_buf[i, at // 2, at % 2, 0] = cal_real.astype(jnp.bfloat16)
                out_buf[i, at // 2, at % 2, 1] = cal_imag.astype(jnp.bfloat16)
        store(i).start()
    for i in range(chunks):
        store(i).wait()


def calibrate(voltages, gains):
    _, _, feeds, channels, samples = voltages.shape
    chunks = 4
    block = channels // chunks
    return pl.pallas_call(
        calibrate_kernel,
        out_shape=jax.ShapeDtypeStruct((channels // 2, 2, 2, feeds, samples), jnp.bfloat16),
        in_specs=[pl.BlockSpec(memory_space=pl.ANY), pl.BlockSpec(memory_space=pltpu.VMEM)],
        out_specs=pl.BlockSpec(memory_space=pl.ANY),
        scratch_shapes=[
            pltpu.VMEM((chunks, 2, feeds, block, samples), jnp.bfloat16),
            pltpu.VMEM((chunks, block // 2, 2, 2, feeds, samples), jnp.bfloat16),
            pltpu.SemaphoreType.DMA((chunks,)),
            pltpu.SemaphoreType.DMA((chunks,)),
        ],
        compiler_params=pltpu.CompilerParams(vmem_limit_bytes=60 * MEGA),
        cost_estimate=pl.CostEstimate(flops=2**29, bytes_accessed=4 * MEGA, transcendentals=0),
        name="calibrate",
    )(voltages, gains)


def beams_kernel(turned_ref, lookup_ref, table_ref, out_ref, place_ref, grid_ref, field_ref):
    sources, channels, _, feeds, samples = turned_ref.shape
    feeds_total = sources * feeds
    cylinders, _, twice, _ = field_ref.shape
    beams = twice // 2
    slot = lax.broadcasted_iota(jnp.int32, (beams, 128), 1)
    for c in range(cylinders):
        rows = pl.ds(c * beams, beams)
        lookup = lookup_ref[rows]
        for at in range(0, feeds_total, 128):
            hit = lookup == slot + at
            place_ref[rows, pl.ds(at, 128)] = hit.astype(jnp.float32).astype(jnp.bfloat16)
    for channel in range(channels):
        for part in range(2):
            own = turned_ref[:, channel, part].reshape(feeds_total, samples)
            placed = jnp.dot(place_ref[...], own, preferred_element_type=jnp.float32).astype(jnp.bfloat16)
            for c in range(cylinders):
                grid_ref[c, pl.ds(part * beams, beams)] = placed[c * beams : c * beams + beams]
        for c in range(cylinders):
            field_ref[c, channel] = jnp.dot(table_ref[channel], grid_ref[c], preferred_element_type=jnp.float32)
    for row in range(0, beams, 8):
        for half in range(samples // 128):
            lanes = pl.ds(half * 128, 128)
            powers = []
            for channel in range(channels):
                re = [field_ref[c, channel, pl.ds(row, 8), lanes] for c in range(4)]
                im = [field_ref[c, channel, pl.ds(beams + row, 8), lanes] for c in range(4)]
                sum_re, sum_im = re[0] + re[2], im[0] + im[2]
                dif_re, dif_im = re[0] - re[2], im[0] - im[2]
                odd_re, odd_im = re[1] + re[3], im[1] + im[3]
                odd_dif_re, odd_dif_im = re[1] - re[3], im[1] - im[3]
                each = [
                    (sum_re + odd_re, sum_im + odd_im),
                    (dif_re + odd_dif_im, dif_im - odd_dif_re),
                    (sum_re - odd_re, sum_im - odd_im),
                    (dif_re - odd_dif_im, dif_im + odd_dif_re),
                ]
                powers.append([a * a + b * b for a, b in each])
            for e in range(4):
                low = jnp.concatenate([powers[0][e][:4], powers[1][e][:4]], axis=0)
                high = jnp.concatenate([powers[0][e][4:], powers[1][e][4:]], axis=0)
                at = e * (beams // 4) + row // 4
                out_ref[at, pl.ds(half * 8, 8)] = low.astype(jnp.bfloat16)
                out_ref[at + 1, pl.ds(half * 8, 8)] = high.astype(jnp.bfloat16)


def form_beams(turned, lookup, table):
    sources, channels, _, feeds, samples = turned.shape
    feeds_total = sources * feeds
    return pl.pallas_call(
        beams_kernel,
        out_shape=jax.ShapeDtypeStruct((feeds_total // 4, 16, 128), jnp.bfloat16),
        in_specs=[pl.BlockSpec(memory_space=pltpu.VMEM)] * 3,
        out_specs=pl.BlockSpec(memory_space=pltpu.VMEM),
        scratch_shapes=[
            pltpu.VMEM((feeds_total, feeds_total), jnp.bfloat16),
            pltpu.VMEM((4, feeds_total // 2, samples), jnp.bfloat16),
            pltpu.VMEM((4, channels, feeds_total // 2, samples), jnp.float32),
        ],
        compiler_params=pltpu.CompilerParams(vmem_limit_bytes=40 * MEGA),
        cost_estimate=pl.CostEstimate(flops=3 * 2**30, bytes_accessed=6 * MEGA, transcendentals=0),
        name="form_beams",
    )(turned, lookup, table)


def total_kernel(sent_ref, out_ref, total_ref):
    block = sent_ref.shape[0]
    total = sent_ref[:, 0].astype(jnp.float32)
    for stream in range(1, 4):
        total += sent_ref[:, stream].astype(jnp.float32)
    for half in range(2):
        total_ref[half] = total[:, half * 8 : half * 8 + 8].reshape(block * 8, 128)
    for beam in range(4):
        for half in range(2):
            rows = total_ref[half, pl.ds(beam, 2 * block, stride=4)]
            out_ref[beam, :, pl.ds(half * 128, 128)] = rows


def add_streams(sent):
    blocks = sent.shape[0]
    block = 16
    return pl.pallas_call(
        total_kernel,
        out_shape=jax.ShapeDtypeStruct((4, 2 * blocks, 256), jnp.float32),
        grid=(blocks // block,),
        in_specs=[pl.BlockSpec((block, 4, 16, 128), lambda i: (i, 0, 0, 0))],
        out_specs=pl.BlockSpec((4, 2 * block, 256), lambda i: (0, i, 0)),
        scratch_shapes=[pltpu.VMEM((2, block * 8, 128), jnp.float32)],
        compiler_params=pltpu.CompilerParams(vmem_limit_bytes=16 * MEGA),
        cost_estimate=pl.CostEstimate(flops=2**20, bytes_accessed=2 * MEGA, transcendentals=0),
        name="add_streams",
    )(sent)


def body(voltages, gains, cylinder_feed_lookup, beam_bins):
    calibrated = calibrate(voltages, gains)
    turned = lax.all_to_all(calibrated, "wide", split_axis=0, concat_axis=0, tiled=True)
    lookup = jnp.broadcast_to(cylinder_feed_lookup[:, None], (cylinder_feed_lookup.shape[0], 128))
    table = dft_table(beam_bins, beam_bins.shape[1])
    power = form_beams(turned, lookup, table)
    sent = lax.all_to_all(power, ("wide", "pol"), split_axis=0, concat_axis=0, tiled=True)
    return add_streams(sent.reshape(-1, 4, 16, 128))


def solution(mesh):
    return jax.shard_map(
        body,
        mesh=mesh,
        in_specs=(
            P(None, "pol", "wide", None, None),
            P(None, None, "wide", None),
            P(),
            P("wide", None),
        ),
        out_specs=P(("wide", "pol"), None, None),
        check_vma=False,
    )
```

```python
import math

import jax
import jax.numpy as jnp
from jax import lax
from jax.experimental import pallas as pl
from jax.experimental.pallas import tpu as pltpu
from jax.sharding import PartitionSpec as P

MEGA = 2**20


def dft_table(bins, feeds_per):
    along = lax.iota(jnp.int32, feeds_per)
    product = bins[:, :, None] * along[None, None, :] % (2 * feeds_per)
    theta = product.astype(jnp.float32) * (math.pi / feeds_per)
    cos_table = jnp.cos(theta).astype(jnp.bfloat16)
    sin_table = jnp.sin(theta).astype(jnp.bfloat16)
    first = jnp.concatenate([cos_table, sin_table], axis=2)
    second = jnp.concatenate([-sin_table, cos_table], axis=2)
    return jnp.concatenate([first, second], axis=1)


def calibrate_kernel(volts_ref, gains_ref, out_ref, in_buf, gain_buf, out_buf, in_sem, gain_sem, out_sem):
    chunks, _, feeds, block, samples = in_buf.shape

    def fetch(i):
        own = volts_ref.at[:, 0, :, pl.ds(i * block, block), :]
        return pltpu.make_async_copy(own, in_buf.at[i], in_sem.at[i])

    def store(i):
        own = out_ref.at[pl.ds(i * block // 2, block // 2)]
        return pltpu.make_async_copy(out_buf.at[i], own, out_sem.at[i])

    gain_copy = pltpu.make_async_copy(gains_ref, gain_buf, gain_sem)
    gain_copy.start()
    for i in range(chunks):
        fetch(i).start()
    row = lax.broadcasted_iota(jnp.int32, (feeds * 16, feeds * 16), 0)
    col = lax.broadcasted_iota(jnp.int32, (feeds * 16, feeds * 16), 1)
    swap = (row // feeds == col % 16) & (row % feeds == col // 16)
    swap = swap.astype(jnp.float32).astype(jnp.bfloat16)
    gain_copy.wait()
    polar = lax.axis_index("pol") // 2
    gain_real = gain_buf[0, polar]
    gain_imag = gain_buf[1, polar]
    for i in range(chunks):
        fetch(i).wait()
        for group in range(block // 16):
            parts = []
            for part in range(2):
                own = in_buf[i, part, :, group * 16 : group * 16 + 16, :].reshape(feeds * 16, samples)
                parts.append(jnp.dot(swap, own, preferred_element_type=jnp.float32))
            for c in range(16):
                at = group * 16 + c
                channel = i * block + at
                own_real = gain_real[:, channel : channel + 1]
                own_imag = gain_imag[:, channel : channel + 1]
                volt_real = parts[0][c * feeds : c * feeds + feeds]
                volt_imag = parts[1][c * feeds : c * feeds + feeds]
                cal_real = own_real * volt_real - own_imag * volt_imag
                cal_imag = own_real * volt_imag + own_imag * volt_real
                out_buf[i, at // 2, at % 2, 0] = cal_real.astype(jnp.bfloat16)
                out_buf[i, at // 2, at % 2, 1] = cal_imag.astype(jnp.bfloat16)
        store(i).start()
    for i in range(chunks):
        store(i).wait()


def calibrate(voltages, gains):
    _, _, feeds, channels, samples = voltages.shape
    chunks = 4
    block = channels // chunks
    return pl.pallas_call(
        calibrate_kernel,
        out_shape=jax.ShapeDtypeStruct((channels // 2, 2, 2, feeds, samples), jnp.bfloat16),
        in_specs=[pl.BlockSpec(memory_space=pl.ANY)] * 2,
        out_specs=pl.BlockSpec(memory_space=pl.ANY),
        scratch_shapes=[
            pltpu.VMEM((chunks, 2, feeds, block, samples), jnp.bfloat16),
            pltpu.VMEM(gains.shape, jnp.float32),
            pltpu.VMEM((chunks, block // 2, 2, 2, feeds, samples), jnp.bfloat16),
            pltpu.SemaphoreType.DMA((chunks,)),
            pltpu.SemaphoreType.DMA,
            pltpu.SemaphoreType.DMA((chunks,)),
        ],
        compiler_params=pltpu.CompilerParams(vmem_limit_bytes=60 * MEGA),
        cost_estimate=pl.CostEstimate(flops=2**29, bytes_accessed=4 * MEGA, transcendentals=0),
        name="calibrate",
    )(voltages, gains)


def beam_powers(real_parts, imag_parts):
    sum_re, sum_im = real_parts[0] + real_parts[2], imag_parts[0] + imag_parts[2]
    dif_re, dif_im = real_parts[0] - real_parts[2], imag_parts[0] - imag_parts[2]
    odd_re, odd_im = real_parts[1] + real_parts[3], imag_parts[1] + imag_parts[3]
    odd_dif_re, odd_dif_im = real_parts[1] - real_parts[3], imag_parts[1] - imag_parts[3]
    each = [
        (sum_re + odd_re, sum_im + odd_im),
        (dif_re + odd_dif_im, dif_im - odd_dif_re),
        (sum_re - odd_re, sum_im - odd_im),
        (dif_re - odd_dif_im, dif_im + odd_dif_re),
    ]
    return [a * a + b * b for a, b in each]


def beams_kernel(turned_ref, lookup_ref, table_ref, out_ref, place_ref, grid_ref):
    sources, channels, _, feeds, samples = turned_ref.shape
    feeds_total = sources * feeds
    cylinders = grid_ref.shape[1]
    beams = feeds_total // cylinders
    slot = lax.broadcasted_iota(jnp.int32, (beams, 128), 1)
    for c in range(cylinders):
        rows = pl.ds(c * beams, beams)
        lookup = lookup_ref[rows]
        for at in range(0, feeds_total, 128):
            hit = lookup == slot + at
            place_ref[rows, pl.ds(at, 128)] = hit.astype(jnp.float32).astype(jnp.bfloat16)
    fields = []
    for channel in range(channels):
        for part in range(2):
            own = turned_ref[:, channel, part].reshape(feeds_total, samples)
            placed = jnp.dot(place_ref[...], own, preferred_element_type=jnp.float32).astype(jnp.bfloat16)
            for c in range(cylinders):
                grid_ref[channel, c, pl.ds(part * beams, beams)] = placed[c * beams : c * beams + beams]
        fields.append([
            jnp.dot(table_ref[channel], grid_ref[channel, c], preferred_element_type=jnp.float32)
            for c in range(cylinders)
        ])
    for channel in range(channels):
        field = fields[channel]
        for row in range(0, beams, 8):
            halves = []
            for at in range(0, samples, 128):
                re = [field[c][row : row + 8, at : at + 128] for c in range(cylinders)]
                im = [field[c][beams + row : beams + row + 8, at : at + 128] for c in range(cylinders)]
                halves.append(beam_powers(re, im))
            for e in range(cylinders):
                low = jnp.concatenate([halves[0][e][:4], halves[1][e][:4]], axis=0)
                high = jnp.concatenate([halves[0][e][4:], halves[1][e][4:]], axis=0)
                at = e * (beams // 4) + row // 4
                out_ref[at, pl.ds(channel * 8, 8)] = low.astype(jnp.bfloat16)
                out_ref[at + 1, pl.ds(channel * 8, 8)] = high.astype(jnp.bfloat16)


def form_beams(turned, lookup, table):
    sources, channels, _, feeds, samples = turned.shape
    feeds_total = sources * feeds
    return pl.pallas_call(
        beams_kernel,
        out_shape=jax.ShapeDtypeStruct((feeds_total // 4, 16, 128), jnp.bfloat16),
        in_specs=[pl.BlockSpec(memory_space=pltpu.VMEM)] * 3,
        out_specs=pl.BlockSpec(memory_space=pltpu.VMEM),
        scratch_shapes=[
            pltpu.VMEM((feeds_total, feeds_total), jnp.bfloat16),
            pltpu.VMEM((channels, 4, feeds_total // 2, samples), jnp.bfloat16),
        ],
        compiler_params=pltpu.CompilerParams(vmem_limit_bytes=40 * MEGA),
        cost_estimate=pl.CostEstimate(flops=3 * 2**30, bytes_accessed=6 * MEGA, transcendentals=0),
        name="form_beams",
    )(turned, lookup, table)


def total_kernel(sent_ref, out_ref, total_ref, out_buf, out_sem):
    chunks = out_sem.shape[0]
    block = sent_ref.shape[0] // chunks

    def store(i):
        own = pl.ds(i * 2 * block, 2 * block)
        return pltpu.make_async_copy(out_buf.at[:, own], out_ref.at[:, own], out_sem.at[i])

    for i in range(chunks):
        own = [sent_ref[pl.ds(i * block, block), stream].astype(jnp.float32) for stream in range(4)]
        total = (own[0] + own[1]) + (own[2] + own[3])
        total_ref[pl.ds(i * block * 16, block * 16)] = total.reshape(block * 16, 128)
        for beam in range(4):
            for half in range(2):
                rows = total_ref[pl.ds(i * block * 16 + half * 4 + beam, 2 * block, stride=8)]
                out_buf[beam, pl.ds(i * 2 * block, 2 * block), pl.ds(half * 128, 128)] = rows
        store(i).start()
    for i in range(chunks):
        store(i).wait()


def add_streams(sent):
    blocks = sent.shape[0]
    chunks = 4
    return pl.pallas_call(
        total_kernel,
        out_shape=jax.ShapeDtypeStruct((4, 2 * blocks, 256), jnp.float32),
        in_specs=[pl.BlockSpec(memory_space=pltpu.VMEM)],
        out_specs=pl.BlockSpec(memory_space=pl.ANY),
        scratch_shapes=[
            pltpu.VMEM((blocks * 16, 128), jnp.float32),
            pltpu.VMEM((4, 2 * blocks, 256), jnp.float32),
            pltpu.SemaphoreType.DMA((chunks,)),
        ],
        compiler_params=pltpu.CompilerParams(vmem_limit_bytes=16 * MEGA),
        cost_estimate=pl.CostEstimate(flops=2**20, bytes_accessed=2 * MEGA, transcendentals=0),
        name="add_streams",
    )(sent)


def body(voltages, gains, cylinder_feed_lookup, beam_bins):
    calibrated = calibrate(voltages, gains)
    turned = lax.all_to_all(calibrated, "wide", split_axis=0, concat_axis=0, tiled=True)
    lookup = jnp.broadcast_to(cylinder_feed_lookup[:, None], (cylinder_feed_lookup.shape[0], 128))
    table = dft_table(beam_bins, beam_bins.shape[1])
    power = form_beams(turned, lookup, table)
    sent = lax.all_to_all(power, ("wide", "pol"), split_axis=0, concat_axis=0, tiled=True)
    return add_streams(sent.reshape(-1, 4, 16, 128))


def solution(mesh):
    return jax.shard_map(
        body,
        mesh=mesh,
        in_specs=(
            P(None, "pol", "wide", None, None),
            P(None, None, "wide", None),
            P(),
            P("wide", None),
        ),
        out_specs=P(("wide", "pol"), None, None),
        check_vma=False,
    )
```

```python
import math

import jax
import jax.numpy as jnp
from jax import lax
from jax.experimental import pallas as pl
from jax.experimental.pallas import tpu as pltpu
from jax.sharding import PartitionSpec as P

MEGA = 2**20


def owner_slot(owner):
    x, y, z, core, stream = owner // 64, owner // 16 % 4, owner // 8 % 2, owner // 4 % 2, owner % 4
    return (((z * 4 + stream) * 4 + x) * 4 + y) * 2 + core


def dft_table(bins, feeds_per):
    along = lax.iota(jnp.int32, feeds_per)
    product = bins[:, :, None] * along[None, None, :] % (2 * feeds_per)
    theta = product.astype(jnp.float32) * (math.pi / feeds_per)
    cos_table = jnp.cos(theta).astype(jnp.bfloat16)
    sin_table = jnp.sin(theta).astype(jnp.bfloat16)
    first = jnp.concatenate([cos_table, sin_table], axis=2)
    second = jnp.concatenate([-sin_table, cos_table], axis=2)
    return jnp.concatenate([first, second], axis=1)


def calibrate_kernel(volts_ref, gains_ref, out_ref, in_buf, gain_buf, out_buf, in_sem, gain_sem, out_sem):
    chunks, _, feeds, block, samples = in_buf.shape

    def fetch(i):
        own = volts_ref.at[:, 0, :, pl.ds(i * block, block), :]
        return pltpu.make_async_copy(own, in_buf.at[i], in_sem.at[i])

    def store(i):
        own = out_ref.at[pl.ds(i * block // 2, block // 2)]
        return pltpu.make_async_copy(out_buf.at[i], own, out_sem.at[i])

    gain_copy = pltpu.make_async_copy(gains_ref, gain_buf, gain_sem)
    gain_copy.start()
    for i in range(chunks):
        fetch(i).start()
    row = lax.broadcasted_iota(jnp.int32, (feeds * 16, feeds * 16), 0)
    col = lax.broadcasted_iota(jnp.int32, (feeds * 16, feeds * 16), 1)
    swap = (row // feeds == col % 16) & (row % feeds == col // 16)
    swap = swap.astype(jnp.float32).astype(jnp.bfloat16)
    gain_copy.wait()
    polar = lax.axis_index("pol") // 2
    gain_real = gain_buf[0, polar]
    gain_imag = gain_buf[1, polar]
    for i in range(chunks):
        fetch(i).wait()
        for group in range(block // 16):
            parts = []
            for part in range(2):
                own = in_buf[i, part, :, group * 16 : group * 16 + 16, :].reshape(feeds * 16, samples)
                parts.append(jnp.dot(swap, own, preferred_element_type=jnp.float32))
            for c in range(16):
                at = group * 16 + c
                channel = i * block + at
                own_real = gain_real[:, channel : channel + 1]
                own_imag = gain_imag[:, channel : channel + 1]
                volt_real = parts[0][c * feeds : c * feeds + feeds]
                volt_imag = parts[1][c * feeds : c * feeds + feeds]
                cal_real = own_real * volt_real - own_imag * volt_imag
                cal_imag = own_real * volt_imag + own_imag * volt_real
                out_buf[i, at // 2, at % 2, 0] = cal_real.astype(jnp.bfloat16)
                out_buf[i, at // 2, at % 2, 1] = cal_imag.astype(jnp.bfloat16)
        store(i).start()
    for i in range(chunks):
        store(i).wait()


def calibrate(voltages, gains):
    _, _, feeds, channels, samples = voltages.shape
    chunks = 2
    block = channels // chunks
    return pl.pallas_call(
        calibrate_kernel,
        out_shape=jax.ShapeDtypeStruct((channels // 2, 2, 2, feeds, samples), jnp.bfloat16),
        in_specs=[pl.BlockSpec(memory_space=pl.ANY)] * 2,
        out_specs=pl.BlockSpec(memory_space=pl.ANY),
        scratch_shapes=[
            pltpu.VMEM((chunks, 2, feeds, block, samples), jnp.bfloat16),
            pltpu.VMEM(gains.shape, jnp.float32),
            pltpu.VMEM((chunks, block // 2, 2, 2, feeds, samples), jnp.bfloat16),
            pltpu.SemaphoreType.DMA((chunks,)),
            pltpu.SemaphoreType.DMA,
            pltpu.SemaphoreType.DMA((chunks,)),
        ],
        compiler_params=pltpu.CompilerParams(vmem_limit_bytes=60 * MEGA),
        cost_estimate=pl.CostEstimate(flops=2**29, bytes_accessed=4 * MEGA, transcendentals=0),
        name="calibrate",
    )(voltages, gains)


def beam_powers(real_parts, imag_parts):
    sum_re, sum_im = real_parts[0] + real_parts[2], imag_parts[0] + imag_parts[2]
    dif_re, dif_im = real_parts[0] - real_parts[2], imag_parts[0] - imag_parts[2]
    odd_re, odd_im = real_parts[1] + real_parts[3], imag_parts[1] + imag_parts[3]
    odd_dif_re, odd_dif_im = real_parts[1] - real_parts[3], imag_parts[1] - imag_parts[3]
    each = [
        (sum_re + odd_re, sum_im + odd_im),
        (dif_re + odd_dif_im, dif_im - odd_dif_re),
        (sum_re - odd_re, sum_im - odd_im),
        (dif_re - odd_dif_im, dif_im + odd_dif_re),
    ]
    return [a * a + b * b for a, b in each]


def beams_kernel(turned_ref, lookup_ref, table_ref, out_ref, place_ref, grid_ref):
    sources, channels, _, feeds, samples = turned_ref.shape
    feeds_total = sources * feeds
    cylinders = grid_ref.shape[1]
    beams = feeds_total // cylinders
    slot = lax.broadcasted_iota(jnp.int32, (beams, 128), 1)
    for c in range(cylinders):
        rows = pl.ds(c * beams, beams)
        lookup = lookup_ref[rows]
        for at in range(0, feeds_total, 128):
            hit = lookup == slot + at
            place_ref[rows, pl.ds(at, 128)] = hit.astype(jnp.float32).astype(jnp.bfloat16)
    fields = []
    for channel in range(channels):
        for part in range(2):
            own = turned_ref[:, channel, part].reshape(feeds_total, samples)
            placed = jnp.dot(place_ref[...], own, preferred_element_type=jnp.float32).astype(jnp.bfloat16)
            for c in range(cylinders):
                grid_ref[channel, c, pl.ds(part * beams, beams)] = placed[c * beams : c * beams + beams]
        fields.append([
            jnp.dot(table_ref[channel], grid_ref[channel, c], preferred_element_type=jnp.float32)
            for c in range(cylinders)
        ])
    for channel in range(channels):
        field = fields[channel]
        for row in range(0, beams, 8):
            halves = []
            for at in range(0, samples, 128):
                re = [field[c][row : row + 8, at : at + 128] for c in range(cylinders)]
                im = [field[c][beams + row : beams + row + 8, at : at + 128] for c in range(cylinders)]
                halves.append(beam_powers(re, im))
            for e in range(cylinders):
                low = jnp.concatenate([halves[0][e][:4], halves[1][e][:4]], axis=0)
                high = jnp.concatenate([halves[0][e][4:], halves[1][e][4:]], axis=0)
                at = e * (beams // 4) + row // 4
                out_ref[owner_slot(at), pl.ds(channel * 8, 8)] = low.astype(jnp.bfloat16)
                out_ref[owner_slot(at + 1), pl.ds(channel * 8, 8)] = high.astype(jnp.bfloat16)


def form_beams(turned, lookup, table):
    sources, channels, _, feeds, samples = turned.shape
    feeds_total = sources * feeds
    return pl.pallas_call(
        beams_kernel,
        out_shape=jax.ShapeDtypeStruct((feeds_total // 4, 16, 128), jnp.bfloat16),
        in_specs=[pl.BlockSpec(memory_space=pltpu.VMEM)] * 3,
        out_specs=pl.BlockSpec(memory_space=pltpu.VMEM),
        scratch_shapes=[
            pltpu.VMEM((feeds_total, feeds_total), jnp.bfloat16),
            pltpu.VMEM((channels, 4, feeds_total // 2, samples), jnp.bfloat16),
        ],
        compiler_params=pltpu.CompilerParams(vmem_limit_bytes=40 * MEGA),
        cost_estimate=pl.CostEstimate(flops=3 * 2**30, bytes_accessed=6 * MEGA, transcendentals=0),
        name="form_beams",
    )(turned, lookup, table)


def total_kernel(sent_ref, out_ref, total_ref, out_buf, out_sem):
    chunks = out_sem.shape[0]
    block = total_ref.shape[0] // 16 // chunks

    def store(i):
        own = pl.ds(i * 2 * block, 2 * block)
        return pltpu.make_async_copy(out_buf.at[:, own], out_ref.at[:, own], out_sem.at[i])

    for i in range(chunks):
        for source in range(i * block, i * block + block, 2):
            own = [
                sent_ref[pl.ds(owner_slot(source * 4 + stream), 2)].astype(jnp.float32) for stream in range(4)
            ]
            total = (own[0] + own[1]) + (own[2] + own[3])
            total_ref[pl.ds(source * 16, 32)] = total.reshape(32, 128)
        for beam in range(4):
            for half in range(2):
                rows = total_ref[pl.ds(i * block * 16 + half * 4 + beam, 2 * block, stride=8)]
                out_buf[beam, pl.ds(i * 2 * block, 2 * block), pl.ds(half * 128, 128)] = rows
        store(i).start()
    for i in range(chunks):
        store(i).wait()


def add_streams(sent):
    blocks = sent.shape[0] // 4
    chunks = 4
    return pl.pallas_call(
        total_kernel,
        out_shape=jax.ShapeDtypeStruct((4, 2 * blocks, 256), jnp.float32),
        in_specs=[pl.BlockSpec(memory_space=pltpu.VMEM)],
        out_specs=pl.BlockSpec(memory_space=pl.ANY),
        scratch_shapes=[
            pltpu.VMEM((blocks * 16, 128), jnp.float32),
            pltpu.VMEM((4, 2 * blocks, 256), jnp.float32),
            pltpu.SemaphoreType.DMA((chunks,)),
        ],
        compiler_params=pltpu.CompilerParams(vmem_limit_bytes=16 * MEGA),
        cost_estimate=pl.CostEstimate(flops=2**20, bytes_accessed=2 * MEGA, transcendentals=0),
        name="add_streams",
    )(sent)


def body(voltages, gains, cylinder_feed_lookup, beam_bins):
    calibrated = calibrate(voltages, gains)
    turned = lax.all_to_all(calibrated, "wide", split_axis=0, concat_axis=0, tiled=True)
    lookup = jnp.broadcast_to(cylinder_feed_lookup[:, None], (cylinder_feed_lookup.shape[0], 128))
    table = dft_table(beam_bins, beam_bins.shape[1])
    power = form_beams(turned, lookup, table)
    owners = power.shape[0]
    order = sorted(range(owners), key=owner_slot)
    sent = lax.all_to_all(
        power, ("wide", "pol"), split_axis=0, concat_axis=0, axis_index_groups=[order], tiled=True
    )
    return add_streams(sent)


def solution(mesh):
    return jax.shard_map(
        body,
        mesh=mesh,
        in_specs=(
            P(None, "pol", "wide", None, None),
            P(None, None, "wide", None),
            P(),
            P("wide", None),
        ),
        out_specs=P(("wide", "pol"), None, None),
        check_vma=False,
    )
```

```python
import itertools
import math

import jax
import jax.numpy as jnp
from jax import lax
from jax.experimental import pallas as pl
from jax.experimental.pallas import tpu as pltpu
from jax.sharding import PartitionSpec as P

MEGA = 2**20


def dft_table(bins, feeds_per):
    along = lax.iota(jnp.int32, feeds_per)
    product = bins[:, :, None] * along[None, None, :] % (2 * feeds_per)
    theta = product.astype(jnp.float32) * (math.pi / feeds_per)
    cos_table = jnp.cos(theta).astype(jnp.bfloat16)
    sin_table = jnp.sin(theta).astype(jnp.bfloat16)
    first = jnp.concatenate([cos_table, sin_table], axis=2)
    second = jnp.concatenate([-sin_table, cos_table], axis=2)
    return jnp.concatenate([first, second], axis=1)


def calibrate_kernel(volts_ref, gains_ref, out_ref, in_buf, gain_buf, out_buf, in_sem, gain_sem, out_sem):
    chunks, _, feeds, block, samples = in_buf.shape

    def fetch(i):
        own = volts_ref.at[:, 0, :, pl.ds(i * block, block), :]
        return pltpu.make_async_copy(own, in_buf.at[i], in_sem.at[i])

    def store(i):
        own = out_ref.at[pl.ds(i * block // 2, block // 2)]
        return pltpu.make_async_copy(out_buf.at[i], own, out_sem.at[i])

    gain_copy = pltpu.make_async_copy(gains_ref, gain_buf, gain_sem)
    gain_copy.start()
    for i in range(chunks):
        fetch(i).start()
    row = lax.broadcasted_iota(jnp.int32, (feeds * 16, feeds * 16), 0)
    col = lax.broadcasted_iota(jnp.int32, (feeds * 16, feeds * 16), 1)
    swap = (row // feeds == col % 16) & (row % feeds == col // 16)
    swap = swap.astype(jnp.float32).astype(jnp.bfloat16)
    gain_copy.wait()
    polar = lax.axis_index("pol") // 2
    gain_real = gain_buf[0, polar]
    gain_imag = gain_buf[1, polar]
    for i in range(chunks):
        fetch(i).wait()
        for group in range(block // 16):
            parts = []
            for part in range(2):
                own = in_buf[i, part, :, group * 16 : group * 16 + 16, :].reshape(feeds * 16, samples)
                parts.append(jnp.dot(swap, own, preferred_element_type=jnp.float32))
            for c in range(16):
                at = group * 16 + c
                channel = i * block + at
                own_real = gain_real[:, channel : channel + 1]
                own_imag = gain_imag[:, channel : channel + 1]
                volt_real = parts[0][c * feeds : c * feeds + feeds]
                volt_imag = parts[1][c * feeds : c * feeds + feeds]
                cal_real = own_real * volt_real - own_imag * volt_imag
                cal_imag = own_real * volt_imag + own_imag * volt_real
                out_buf[i, at // 2, at % 2, 0] = cal_real.astype(jnp.bfloat16)
                out_buf[i, at // 2, at % 2, 1] = cal_imag.astype(jnp.bfloat16)
        store(i).start()
    for i in range(chunks):
        store(i).wait()


def calibrate(voltages, gains):
    _, _, feeds, channels, samples = voltages.shape
    chunks = 2
    block = channels // chunks
    return pl.pallas_call(
        calibrate_kernel,
        out_shape=jax.ShapeDtypeStruct((channels // 2, 2, 2, feeds, samples), jnp.bfloat16),
        in_specs=[pl.BlockSpec(memory_space=pl.ANY)] * 2,
        out_specs=pl.BlockSpec(memory_space=pl.ANY),
        scratch_shapes=[
            pltpu.VMEM((chunks, 2, feeds, block, samples), jnp.bfloat16),
            pltpu.VMEM(gains.shape, jnp.float32),
            pltpu.VMEM((chunks, block // 2, 2, 2, feeds, samples), jnp.bfloat16),
            pltpu.SemaphoreType.DMA((chunks,)),
            pltpu.SemaphoreType.DMA,
            pltpu.SemaphoreType.DMA((chunks,)),
        ],
        compiler_params=pltpu.CompilerParams(vmem_limit_bytes=60 * MEGA),
        cost_estimate=pl.CostEstimate(flops=2**29, bytes_accessed=4 * MEGA, transcendentals=0),
        name="calibrate",
    )(voltages, gains)


def beam_powers(real_parts, imag_parts):
    sum_re, sum_im = real_parts[0] + real_parts[2], imag_parts[0] + imag_parts[2]
    dif_re, dif_im = real_parts[0] - real_parts[2], imag_parts[0] - imag_parts[2]
    odd_re, odd_im = real_parts[1] + real_parts[3], imag_parts[1] + imag_parts[3]
    odd_dif_re, odd_dif_im = real_parts[1] - real_parts[3], imag_parts[1] - imag_parts[3]
    each = [
        (sum_re + odd_re, sum_im + odd_im),
        (dif_re + odd_dif_im, dif_im - odd_dif_re),
        (sum_re - odd_re, sum_im - odd_im),
        (dif_re - odd_dif_im, dif_im + odd_dif_re),
    ]
    return [a * a + b * b for a, b in each]


def one_hot(hit):
    return hit.astype(jnp.float32).astype(jnp.bfloat16)


def route_kernel(rows_ref, lookup_ref, table_ref, swap_ref, choice_ref, spread_ref):
    groups, size = rows_ref.shape
    column = lax.broadcasted_iota(jnp.int32, (size, 128), 0)
    lane = lax.broadcasted_iota(jnp.int32, (size, 128), 1)
    block = [rows_ref[c : c + 1] >> 8 for c in range(groups)]
    rank, left = [], [[None] * groups for _ in range(groups)]
    for c in range(groups):
        own = lookup_ref[pl.ds(c * size, size)] >> 8
        parts = []
        for at in range(0, size, 128):
            before = (own == block[c][:, at : at + 128]) & (column < lane + at)
            parts.append(jnp.sum(before.astype(jnp.int32), axis=0, keepdims=True))
        rank.append(jnp.concatenate(parts, axis=1))
        for b in range(groups):
            left[b][c] = jnp.sum((block[c] == b).astype(jnp.int32))
    used = [[0] * groups for _ in range(groups)]
    place = [jnp.zeros((1, size), jnp.int32) for _ in range(groups)]
    choice = [jnp.zeros((size, 128), jnp.int32) for _ in range(groups)]
    start = 0
    for target in itertools.permutations(range(groups)):
        weight = left[0][target[0]]
        for b in range(1, groups):
            weight = jnp.minimum(weight, left[b][target[b]])
        inside = (column >= start) & (column < start + weight)
        for b in range(groups):
            c = target[b]
            low = used[b][c]
            hit = (block[c] == b) & (rank[c] >= low) & (rank[c] < low + weight)
            place[c] = jnp.where(hit, rank[c] + (start - low), place[c])
            choice[c] = jnp.where(inside, b, choice[c])
            left[b][c] = left[b][c] - weight
            used[b][c] = low + weight
        start = start + weight
    down = lax.broadcasted_iota(jnp.int32, (size, size), 0)
    across = lax.broadcasted_iota(jnp.int32, (size, size), 1)
    for c in range(groups):
        choice_ref[c] = choice[c]
        upright = jnp.sum(jnp.where(down == across, place[c], 0), axis=1, keepdims=True)
        order = one_hot(upright == across)
        for channel in range(table_ref.shape[0]):
            for part in range(2):
                lanes = pl.ds(part * size, size)
                own = jnp.dot(table_ref[channel, :, lanes], order, preferred_element_type=jnp.float32)
                spread_ref[channel, c, :, lanes] = own.astype(jnp.bfloat16)
    for b in range(groups):
        total = jnp.zeros((size, size), jnp.float32)
        for c in range(groups):
            target = one_hot((place[c] == down) & (block[c] == b))
            own = lookup_ref[pl.ds(c * size, size)]
            source = jnp.concatenate([own == lane + (b * size + at) for at in range(0, size, 128)], axis=1)
            total += jnp.dot(target, one_hot(source), preferred_element_type=jnp.float32)
        swap_ref[b] = total.astype(jnp.bfloat16)


def route(rows, lookup, table):
    groups, size = rows.shape
    channels, twice, _ = table.shape
    return pl.pallas_call(
        route_kernel,
        out_shape=(
            jax.ShapeDtypeStruct((groups, size, size), jnp.bfloat16),
            jax.ShapeDtypeStruct((groups, size, 128), jnp.int32),
            jax.ShapeDtypeStruct((channels, groups, twice, twice), jnp.bfloat16),
        ),
        in_specs=[pl.BlockSpec(memory_space=pltpu.VMEM)] * 3,
        out_specs=(pl.BlockSpec(memory_space=pltpu.VMEM),) * 3,
        compiler_params=pltpu.CompilerParams(vmem_limit_bytes=24 * MEGA),
        cost_estimate=pl.CostEstimate(flops=2 * 2**30, bytes_accessed=8 * MEGA, transcendentals=0),
        name="route",
    )(rows, lookup, table)


def beams_kernel(turned_ref, swap_ref, choice_ref, spread_ref, out_ref, grid_ref):
    sources, channels, _, feeds, samples = turned_ref.shape
    feeds_total = sources * feeds
    cylinders, size, _ = swap_ref.shape
    fields = []
    for channel in range(channels):
        for part in range(2):
            own = turned_ref[:, channel, part].reshape(feeds_total, samples)
            moved = [
                jnp.dot(swap_ref[b], own[b * size : b * size + size], preferred_element_type=jnp.float32)
                for b in range(cylinders)
            ]
            for at in range(0, samples, 128):
                for c in range(cylinders):
                    pick = choice_ref[c]
                    got = moved[3][:, at : at + 128]
                    for b in range(3):
                        got = jnp.where(pick == b, moved[b][:, at : at + 128], got)
                    grid_ref[channel, c, pl.ds(part * size, size), pl.ds(at, 128)] = got.astype(jnp.bfloat16)
        fields.append([
            jnp.dot(spread_ref[channel, c], grid_ref[channel, c], preferred_element_type=jnp.float32)
            for c in range(cylinders)
        ])
    for channel in range(channels):
        field = fields[channel]
        for row in range(0, size, 8):
            halves = []
            for at in range(0, samples, 128):
                re = [field[c][row : row + 8, at : at + 128] for c in range(cylinders)]
                im = [field[c][size + row : size + row + 8, at : at + 128] for c in range(cylinders)]
                halves.append(beam_powers(re, im))
            for e in range(cylinders):
                low = jnp.concatenate([halves[0][e][:4], halves[1][e][:4]], axis=0)
                high = jnp.concatenate([halves[0][e][4:], halves[1][e][4:]], axis=0)
                at = e * (size // 4) + row // 4
                out_ref[at, pl.ds(channel * 8, 8)] = low.astype(jnp.bfloat16)
                out_ref[at + 1, pl.ds(channel * 8, 8)] = high.astype(jnp.bfloat16)


def form_beams(turned, swap, choice, spread):
    sources, channels, _, feeds, samples = turned.shape
    feeds_total = sources * feeds
    return pl.pallas_call(
        beams_kernel,
        out_shape=jax.ShapeDtypeStruct((feeds_total // 4, 16, 128), jnp.bfloat16),
        in_specs=[pl.BlockSpec(memory_space=pltpu.VMEM)] * 4,
        out_specs=pl.BlockSpec(memory_space=pltpu.VMEM),
        scratch_shapes=[pltpu.VMEM((channels, 4, feeds_total // 2, samples), jnp.bfloat16)],
        compiler_params=pltpu.CompilerParams(vmem_limit_bytes=30 * MEGA),
        cost_estimate=pl.CostEstimate(flops=3 * 2**29, bytes_accessed=8 * MEGA, transcendentals=0),
        name="form_beams",
    )(turned, swap, choice, spread)


def total_kernel(sent_ref, out_ref, total_ref, out_buf, out_sem):
    chunks = out_sem.shape[0]
    block = sent_ref.shape[0] // chunks

    def store(i):
        own = pl.ds(i * 2 * block, 2 * block)
        return pltpu.make_async_copy(out_buf.at[:, own], out_ref.at[:, own], out_sem.at[i])

    for i in range(chunks):
        own = [sent_ref[pl.ds(i * block, block), stream].astype(jnp.float32) for stream in range(4)]
        total = (own[0] + own[1]) + (own[2] + own[3])
        total_ref[pl.ds(i * block * 16, block * 16)] = total.reshape(block * 16, 128)
        for beam in range(4):
            for half in range(2):
                rows = total_ref[pl.ds(i * block * 16 + half * 4 + beam, 2 * block, stride=8)]
                out_buf[beam, pl.ds(i * 2 * block, 2 * block), pl.ds(half * 128, 128)] = rows
        store(i).start()
    for i in range(chunks):
        store(i).wait()


def add_streams(sent):
    blocks = sent.shape[0]
    chunks = 4
    return pl.pallas_call(
        total_kernel,
        out_shape=jax.ShapeDtypeStruct((4, 2 * blocks, 256), jnp.float32),
        in_specs=[pl.BlockSpec(memory_space=pltpu.VMEM)],
        out_specs=pl.BlockSpec(memory_space=pl.ANY),
        scratch_shapes=[
            pltpu.VMEM((blocks * 16, 128), jnp.float32),
            pltpu.VMEM((4, 2 * blocks, 256), jnp.float32),
            pltpu.SemaphoreType.DMA((chunks,)),
        ],
        compiler_params=pltpu.CompilerParams(vmem_limit_bytes=16 * MEGA),
        cost_estimate=pl.CostEstimate(flops=2**20, bytes_accessed=2 * MEGA, transcendentals=0),
        name="add_streams",
    )(sent)


def body(voltages, gains, cylinder_feed_lookup, beam_bins):
    calibrated = calibrate(voltages, gains)
    turned = lax.all_to_all(calibrated, "wide", split_axis=0, concat_axis=0, tiled=True)
    lookup = jnp.broadcast_to(cylinder_feed_lookup[:, None], (cylinder_feed_lookup.shape[0], 128))
    table = dft_table(beam_bins, beam_bins.shape[1])
    swap, choice, spread = route(cylinder_feed_lookup.reshape(4, -1), lookup, table)
    power = form_beams(turned, swap, choice, spread)
    sent = lax.all_to_all(power, ("wide", "pol"), split_axis=0, concat_axis=0, tiled=True)
    return add_streams(sent.reshape(-1, 4, 16, 128))


def solution(mesh):
    return jax.shard_map(
        body,
        mesh=mesh,
        in_specs=(
            P(None, "pol", "wide", None, None),
            P(None, None, "wide", None),
            P(),
            P("wide", None),
        ),
        out_specs=P(("wide", "pol"), None, None),
        check_vma=False,
    )
```

```python
import itertools
import math

import jax
import jax.numpy as jnp
from jax import lax
from jax.experimental import pallas as pl
from jax.experimental.pallas import tpu as pltpu
from jax.sharding import PartitionSpec as P

MEGA = 2**20


def dft_table(bins, feeds_per):
    along = lax.iota(jnp.int32, feeds_per)
    product = bins[:, :, None] * along[None, None, :] % (2 * feeds_per)
    theta = product.astype(jnp.float32) * (math.pi / feeds_per)
    cos_table = jnp.cos(theta).astype(jnp.bfloat16)
    sin_table = jnp.sin(theta).astype(jnp.bfloat16)
    return jnp.concatenate([cos_table, sin_table], axis=1)


def calibrate_kernel(volts_ref, gains_ref, out_ref, in_buf, gain_buf, out_buf, in_sem, gain_sem, out_sem):
    chunks, _, feeds, block, samples = in_buf.shape

    def fetch(i):
        own = volts_ref.at[:, 0, :, pl.ds(i * block, block), :]
        return pltpu.make_async_copy(own, in_buf.at[i], in_sem.at[i])

    def store(i):
        own = out_ref.at[pl.ds(i * block // 2, block // 2)]
        return pltpu.make_async_copy(out_buf.at[i], own, out_sem.at[i])

    gain_copy = pltpu.make_async_copy(gains_ref, gain_buf, gain_sem)
    gain_copy.start()
    for i in range(chunks):
        fetch(i).start()
    row = lax.broadcasted_iota(jnp.int32, (feeds * 16, feeds * 16), 0)
    col = lax.broadcasted_iota(jnp.int32, (feeds * 16, feeds * 16), 1)
    swap = (row // feeds == col % 16) & (row % feeds == col // 16)
    swap = swap.astype(jnp.float32).astype(jnp.bfloat16)
    gain_copy.wait()
    polar = lax.axis_index("pol") // 2
    gain_real = gain_buf[0, polar]
    gain_imag = gain_buf[1, polar]
    for i in range(chunks):
        fetch(i).wait()
        for group in range(block // 16):
            parts = []
            for part in range(2):
                own = in_buf[i, part, :, group * 16 : group * 16 + 16, :].reshape(feeds * 16, samples)
                parts.append(jnp.dot(swap, own, preferred_element_type=jnp.float32))
            for c in range(16):
                at = group * 16 + c
                channel = i * block + at
                own_real = gain_real[:, channel : channel + 1]
                own_imag = gain_imag[:, channel : channel + 1]
                volt_real = parts[0][c * feeds : c * feeds + feeds]
                volt_imag = parts[1][c * feeds : c * feeds + feeds]
                cal_real = own_real * volt_real - own_imag * volt_imag
                cal_imag = own_real * volt_imag + own_imag * volt_real
                out_buf[i, at // 2, at % 2, 0] = cal_real.astype(jnp.bfloat16)
                out_buf[i, at // 2, at % 2, 1] = cal_imag.astype(jnp.bfloat16)
        store(i).start()
    for i in range(chunks):
        store(i).wait()


def calibrate(voltages, gains):
    _, _, feeds, channels, samples = voltages.shape
    chunks = 2
    block = channels // chunks
    return pl.pallas_call(
        calibrate_kernel,
        out_shape=jax.ShapeDtypeStruct((channels // 2, 2, 2, feeds, samples), jnp.bfloat16),
        in_specs=[pl.BlockSpec(memory_space=pl.ANY)] * 2,
        out_specs=pl.BlockSpec(memory_space=pl.ANY),
        scratch_shapes=[
            pltpu.VMEM((chunks, 2, feeds, block, samples), jnp.bfloat16),
            pltpu.VMEM(gains.shape, jnp.float32),
            pltpu.VMEM((chunks, block // 2, 2, 2, feeds, samples), jnp.bfloat16),
            pltpu.SemaphoreType.DMA((chunks,)),
            pltpu.SemaphoreType.DMA,
            pltpu.SemaphoreType.DMA((chunks,)),
        ],
        compiler_params=pltpu.CompilerParams(vmem_limit_bytes=60 * MEGA),
        cost_estimate=pl.CostEstimate(flops=2**29, bytes_accessed=4 * MEGA, transcendentals=0),
        name="calibrate",
    )(voltages, gains)


def beam_powers(real_parts, imag_parts):
    sum_re, sum_im = real_parts[0] + real_parts[2], imag_parts[0] + imag_parts[2]
    dif_re, dif_im = real_parts[0] - real_parts[2], imag_parts[0] - imag_parts[2]
    odd_re, odd_im = real_parts[1] + real_parts[3], imag_parts[1] + imag_parts[3]
    odd_dif_re, odd_dif_im = real_parts[1] - real_parts[3], imag_parts[1] - imag_parts[3]
    each = [
        (sum_re + odd_re, sum_im + odd_im),
        (dif_re + odd_dif_im, dif_im - odd_dif_re),
        (sum_re - odd_re, sum_im - odd_im),
        (dif_re - odd_dif_im, dif_im + odd_dif_re),
    ]
    return [a * a + b * b for a, b in each]


def one_hot(hit):
    return hit.astype(jnp.float32).astype(jnp.bfloat16)


def route_kernel(rows_ref, lookup_ref, table_ref, swap_ref, choice_ref, first_ref, second_ref, second_buf, sem):
    groups, size = rows_ref.shape
    column = lax.broadcasted_iota(jnp.int32, (size, 128), 0)
    lane = lax.broadcasted_iota(jnp.int32, (size, 128), 1)
    block = [rows_ref[c : c + 1] >> 8 for c in range(groups)]
    rank, left = [], [[None] * groups for _ in range(groups)]
    for c in range(groups):
        own = lookup_ref[pl.ds(c * size, size)] >> 8
        parts = []
        for at in range(0, size, 128):
            before = (own == block[c][:, at : at + 128]) & (column < lane + at)
            parts.append(jnp.sum(before.astype(jnp.int32), axis=0, keepdims=True))
        rank.append(jnp.concatenate(parts, axis=1))
        for b in range(groups):
            left[b][c] = jnp.sum((block[c] == b).astype(jnp.int32))
    used = [[0] * groups for _ in range(groups)]
    place = [jnp.zeros((1, size), jnp.int32) for _ in range(groups)]
    choice = [jnp.zeros((size, 128), jnp.int32) for _ in range(groups)]
    start = 0
    for target in itertools.permutations(range(groups)):
        weight = left[0][target[0]]
        for b in range(1, groups):
            weight = jnp.minimum(weight, left[b][target[b]])
        inside = (column >= start) & (column < start + weight)
        for b in range(groups):
            c = target[b]
            low = used[b][c]
            hit = (block[c] == b) & (rank[c] >= low) & (rank[c] < low + weight)
            place[c] = jnp.where(hit, rank[c] + (start - low), place[c])
            choice[c] = jnp.where(inside, b, choice[c])
            left[b][c] = left[b][c] - weight
            used[b][c] = low + weight
        start = start + weight
    down = lax.broadcasted_iota(jnp.int32, (size, size), 0)
    across = lax.broadcasted_iota(jnp.int32, (size, size), 1)
    code = choice[0]
    for c in range(1, groups):
        code = code + choice[c] * 4**c
    choice_ref[...] = code
    upright = [jnp.sum(jnp.where(down == across, place[c], 0), axis=1, keepdims=True) for c in range(groups)]
    store = pltpu.make_async_copy(second_buf, second_ref.at[0], sem)
    for channel, own_ref in ((1, second_buf), (0, first_ref)):
        for c in range(groups):
            order = one_hot(upright[c] == across)
            own = jnp.dot(table_ref[channel], order, preferred_element_type=jnp.float32)
            own_ref[c] = own.astype(jnp.bfloat16)
        if channel == 1:
            store.start()
    for b in range(groups):
        for at in range(0, size, 128):
            total = jnp.zeros((1, 128), jnp.int32)
            for c in range(groups):
                hit = lookup_ref[pl.ds(c * size, size)] == lane + (b * size + at)
                total += jnp.sum(jnp.where(hit, upright[c], 0), axis=0, keepdims=True)
            swap_ref[pl.ds(b, 1), pl.ds(at, 128)] = total
    store.wait()


def route(rows, lookup, table):
    groups, size = rows.shape
    _, twice, _ = table.shape
    return pl.pallas_call(
        route_kernel,
        out_shape=(
            jax.ShapeDtypeStruct((groups, size), jnp.int32),
            jax.ShapeDtypeStruct((size, 128), jnp.int32),
            jax.ShapeDtypeStruct((groups, twice, size), jnp.bfloat16),
            jax.ShapeDtypeStruct((12, groups, twice, size), jnp.bfloat16),
        ),
        in_specs=[pl.BlockSpec(memory_space=pltpu.VMEM)] * 3,
        out_specs=(pl.BlockSpec(memory_space=pltpu.VMEM),) * 3 + (pl.BlockSpec(memory_space=pl.ANY),),
        scratch_shapes=[pltpu.VMEM((groups, twice, size), jnp.bfloat16), pltpu.SemaphoreType.DMA],
        compiler_params=pltpu.CompilerParams(vmem_limit_bytes=44 * MEGA),
        cost_estimate=pl.CostEstimate(flops=2 * 2**30, bytes_accessed=8 * MEGA, transcendentals=0),
        name="route",
    )(rows, lookup, table)


def beams_kernel(turned_ref, swap_ref, choice_ref, first_ref, second_ref, out_ref, grid_ref, second_buf, sem):
    sources, channels, _, feeds, samples = turned_ref.shape
    feeds_total = sources * feeds
    cylinders, size = swap_ref.shape
    fetch = pltpu.make_async_copy(second_ref.at[0], second_buf, sem)
    fetch.start()
    down = lax.broadcasted_iota(jnp.int32, (size, size), 0)
    swap = [one_hot(swap_ref[b : b + 1] == down) for b in range(cylinders)]
    fields = []
    for channel, table_ref in ((0, first_ref), (1, second_buf)):
        for part in range(2):
            own = turned_ref[:, channel, part].reshape(feeds_total, samples)
            moved = [
                jnp.dot(swap[b], own[b * size : b * size + size], preferred_element_type=jnp.float32)
                for b in range(cylinders)
            ]
            for at in range(0, samples, 128):
                for c in range(cylinders):
                    pick = (choice_ref[...] >> (2 * c)) & 3
                    got = moved[3][:, at : at + 128]
                    for b in range(3):
                        got = jnp.where(pick == b, moved[b][:, at : at + 128], got)
                    grid_ref[channel, c, part, :, pl.ds(at, 128)] = got.astype(jnp.bfloat16)
        if channel == 1:
            fetch.wait()
        field = []
        for c in range(cylinders):
            by_real, by_imag = [
                jnp.dot(table_ref[c], grid_ref[channel, c, part], preferred_element_type=jnp.float32)
                for part in range(2)
            ]
            field.append((by_real[:size] + by_imag[size:], by_imag[:size] - by_real[size:]))
        fields.append(field)
    for channel in range(channels):
        field = fields[channel]
        for row in range(0, size, 8):
            halves = []
            for at in range(0, samples, 128):
                re = [field[c][0][row : row + 8, at : at + 128] for c in range(cylinders)]
                im = [field[c][1][row : row + 8, at : at + 128] for c in range(cylinders)]
                halves.append(beam_powers(re, im))
            for e in range(cylinders):
                low = jnp.concatenate([halves[0][e][:4], halves[1][e][:4]], axis=0)
                high = jnp.concatenate([halves[0][e][4:], halves[1][e][4:]], axis=0)
                at = e * (size // 4) + row // 4
                out_ref[at, pl.ds(channel * 8, 8)] = low.astype(jnp.bfloat16)
                out_ref[at + 1, pl.ds(channel * 8, 8)] = high.astype(jnp.bfloat16)


def form_beams(turned, swap, choice, first, second):
    sources, channels, _, feeds, samples = turned.shape
    feeds_total = sources * feeds
    return pl.pallas_call(
        beams_kernel,
        out_shape=jax.ShapeDtypeStruct((feeds_total // 4, 16, 128), jnp.bfloat16),
        in_specs=[pl.BlockSpec(memory_space=pltpu.VMEM)] * 4 + [pl.BlockSpec(memory_space=pl.ANY)],
        out_specs=pl.BlockSpec(memory_space=pltpu.VMEM),
        scratch_shapes=[
            pltpu.VMEM((channels, 4, 2, feeds_total // 4, samples), jnp.bfloat16),
            pltpu.VMEM(first.shape, jnp.bfloat16),
            pltpu.SemaphoreType.DMA,
        ],
        compiler_params=pltpu.CompilerParams(vmem_limit_bytes=44 * MEGA),
        cost_estimate=pl.CostEstimate(flops=3 * 2**29, bytes_accessed=8 * MEGA, transcendentals=0),
        name="form_beams",
    )(turned, swap, choice, first, second)


def total_kernel(sent_ref, out_ref, total_ref, out_buf, out_sem):
    chunks = out_sem.shape[0]
    block = sent_ref.shape[0] // chunks

    def store(i):
        own = pl.ds(i * 2 * block, 2 * block)
        return pltpu.make_async_copy(out_buf.at[:, own], out_ref.at[:, own], out_sem.at[i])

    for i in range(chunks):
        own = [sent_ref[pl.ds(i * block, block), stream].astype(jnp.float32) for stream in range(4)]
        total = (own[0] + own[1]) + (own[2] + own[3])
        total_ref[pl.ds(i * block * 16, block * 16)] = total.reshape(block * 16, 128)
        for beam in range(4):
            for half in range(2):
                rows = total_ref[pl.ds(i * block * 16 + half * 4 + beam, 2 * block, stride=8)]
                out_buf[beam, pl.ds(i * 2 * block, 2 * block), pl.ds(half * 128, 128)] = rows
        store(i).start()
    for i in range(chunks):
        store(i).wait()


def add_streams(sent):
    blocks = sent.shape[0]
    chunks = 4
    return pl.pallas_call(
        total_kernel,
        out_shape=jax.ShapeDtypeStruct((4, 2 * blocks, 256), jnp.float32),
        in_specs=[pl.BlockSpec(memory_space=pltpu.VMEM)],
        out_specs=pl.BlockSpec(memory_space=pl.ANY),
        scratch_shapes=[
            pltpu.VMEM((blocks * 16, 128), jnp.float32),
            pltpu.VMEM((4, 2 * blocks, 256), jnp.float32),
            pltpu.SemaphoreType.DMA((chunks,)),
        ],
        compiler_params=pltpu.CompilerParams(vmem_limit_bytes=16 * MEGA),
        cost_estimate=pl.CostEstimate(flops=2**20, bytes_accessed=2 * MEGA, transcendentals=0),
        name="add_streams",
    )(sent)


def body(voltages, gains, cylinder_feed_lookup, beam_bins):
    calibrated = calibrate(voltages, gains)
    turned = lax.all_to_all(calibrated, "wide", split_axis=0, concat_axis=0, tiled=True)
    lookup = jnp.broadcast_to(cylinder_feed_lookup[:, None], (cylinder_feed_lookup.shape[0], 128))
    table = dft_table(beam_bins, beam_bins.shape[1])
    swap, choice, first, second = route(cylinder_feed_lookup.reshape(4, -1), lookup, table)
    power = form_beams(turned, swap, choice, first, second)
    sent = lax.all_to_all(power, ("wide", "pol"), split_axis=0, concat_axis=0, tiled=True)
    return add_streams(sent.reshape(-1, 4, 16, 128))


def solution(mesh):
    return jax.shard_map(
        body,
        mesh=mesh,
        in_specs=(
            P(None, "pol", "wide", None, None),
            P(None, None, "wide", None),
            P(),
            P("wide", None),
        ),
        out_specs=P(("wide", "pol"), None, None),
        check_vma=False,
    )
```

```python
import itertools
import math

import jax
import jax.numpy as jnp
from jax import lax
from jax.experimental import pallas as pl
from jax.experimental.pallas import tpu as pltpu
from jax.sharding import PartitionSpec as P

MEGA = 2**20


def owner_slot(owner):
    x, y, z, core, stream = owner // 64, owner // 16 % 4, owner // 8 % 2, owner // 4 % 2, owner % 4
    return (stream * 2 + z) * 32 + (x * 4 + y) * 2 + core


def dft_table(bins, feeds_per):
    along = lax.iota(jnp.int32, feeds_per)
    product = bins[:, :, None] * along[None, None, :] % (2 * feeds_per)
    theta = product.astype(jnp.float32) * (math.pi / feeds_per)
    cos_table = jnp.cos(theta).astype(jnp.bfloat16)
    sin_table = jnp.sin(theta).astype(jnp.bfloat16)
    return jnp.concatenate([cos_table, sin_table], axis=1)


def calibrate_kernel(volts_ref, gains_ref, out_ref, in_buf, gain_buf, out_buf, in_sem, gain_sem, out_sem):
    chunks, _, feeds, block, samples = in_buf.shape

    def fetch(i):
        own = volts_ref.at[:, 0, :, pl.ds(i * block, block), :]
        return pltpu.make_async_copy(own, in_buf.at[i], in_sem.at[i])

    def store(i):
        own = out_ref.at[pl.ds(i * block // 2, block // 2)]
        return pltpu.make_async_copy(out_buf.at[i], own, out_sem.at[i])

    gain_copy = pltpu.make_async_copy(gains_ref, gain_buf, gain_sem)
    gain_copy.start()
    for i in range(chunks):
        fetch(i).start()
    row = lax.broadcasted_iota(jnp.int32, (feeds * 16, feeds * 16), 0)
    col = lax.broadcasted_iota(jnp.int32, (feeds * 16, feeds * 16), 1)
    swap = (row // feeds == col % 16) & (row % feeds == col // 16)
    swap = swap.astype(jnp.float32).astype(jnp.bfloat16)
    gain_copy.wait()
    polar = lax.axis_index("pol") // 2
    gain_real = gain_buf[0, polar]
    gain_imag = gain_buf[1, polar]
    for i in range(chunks):
        fetch(i).wait()
        for group in range(block // 16):
            parts = []
            for part in range(2):
                own = in_buf[i, part, :, group * 16 : group * 16 + 16, :].reshape(feeds * 16, samples)
                parts.append(jnp.dot(swap, own, preferred_element_type=jnp.float32))
            for c in range(16):
                at = group * 16 + c
                channel = i * block + at
                own_real = gain_real[:, channel : channel + 1]
                own_imag = gain_imag[:, channel : channel + 1]
                volt_real = parts[0][c * feeds : c * feeds + feeds]
                volt_imag = parts[1][c * feeds : c * feeds + feeds]
                cal_real = own_real * volt_real - own_imag * volt_imag
                cal_imag = own_real * volt_imag + own_imag * volt_real
                out_buf[i, at // 2, at % 2, 0] = cal_real.astype(jnp.bfloat16)
                out_buf[i, at // 2, at % 2, 1] = cal_imag.astype(jnp.bfloat16)
        store(i).start()
    for i in range(chunks):
        store(i).wait()


def calibrate(voltages, gains):
    _, _, feeds, channels, samples = voltages.shape
    chunks = 2
    block = channels // chunks
    return pl.pallas_call(
        calibrate_kernel,
        out_shape=jax.ShapeDtypeStruct((channels // 2, 2, 2, feeds, samples), jnp.bfloat16),
        in_specs=[pl.BlockSpec(memory_space=pl.ANY)] * 2,
        out_specs=pl.BlockSpec(memory_space=pl.ANY),
        scratch_shapes=[
            pltpu.VMEM((chunks, 2, feeds, block, samples), jnp.bfloat16),
            pltpu.VMEM(gains.shape, jnp.float32),
            pltpu.VMEM((chunks, block // 2, 2, 2, feeds, samples), jnp.bfloat16),
            pltpu.SemaphoreType.DMA((chunks,)),
            pltpu.SemaphoreType.DMA,
            pltpu.SemaphoreType.DMA((chunks,)),
        ],
        compiler_params=pltpu.CompilerParams(vmem_limit_bytes=60 * MEGA),
        cost_estimate=pl.CostEstimate(flops=2**29, bytes_accessed=4 * MEGA, transcendentals=0),
        name="calibrate",
    )(voltages, gains)


def beam_powers(real_parts, imag_parts):
    sum_re, sum_im = real_parts[0] + real_parts[2], imag_parts[0] + imag_parts[2]
    dif_re, dif_im = real_parts[0] - real_parts[2], imag_parts[0] - imag_parts[2]
    odd_re, odd_im = real_parts[1] + real_parts[3], imag_parts[1] + imag_parts[3]
    odd_dif_re, odd_dif_im = real_parts[1] - real_parts[3], imag_parts[1] - imag_parts[3]
    each = [
        (sum_re + odd_re, sum_im + odd_im),
        (dif_re + odd_dif_im, dif_im - odd_dif_re),
        (sum_re - odd_re, sum_im - odd_im),
        (dif_re - odd_dif_im, dif_im + odd_dif_re),
    ]
    return [a * a + b * b for a, b in each]


def one_hot(hit):
    return hit.astype(jnp.float32).astype(jnp.bfloat16)


def route_kernel(rows_ref, lookup_ref, table_ref, swap_ref, choice_ref, first_ref, second_ref, second_buf, sem):
    groups, size = rows_ref.shape
    column = lax.broadcasted_iota(jnp.int32, (size, 128), 0)
    lane = lax.broadcasted_iota(jnp.int32, (size, 128), 1)
    block = [rows_ref[c : c + 1] >> 8 for c in range(groups)]
    rank, left = [], [[None] * groups for _ in range(groups)]
    for c in range(groups):
        own = lookup_ref[pl.ds(c * size, size)] >> 8
        parts = []
        for at in range(0, size, 128):
            before = (own == block[c][:, at : at + 128]) & (column < lane + at)
            parts.append(jnp.sum(before.astype(jnp.int32), axis=0, keepdims=True))
        rank.append(jnp.concatenate(parts, axis=1))
        for b in range(groups):
            left[b][c] = jnp.sum((block[c] == b).astype(jnp.int32))
    used = [[0] * groups for _ in range(groups)]
    place = [jnp.zeros((1, size), jnp.int32) for _ in range(groups)]
    choice = [jnp.zeros((size, 128), jnp.int32) for _ in range(groups)]
    start = 0
    for target in itertools.permutations(range(groups)):
        weight = left[0][target[0]]
        for b in range(1, groups):
            weight = jnp.minimum(weight, left[b][target[b]])
        inside = (column >= start) & (column < start + weight)
        for b in range(groups):
            c = target[b]
            low = used[b][c]
            hit = (block[c] == b) & (rank[c] >= low) & (rank[c] < low + weight)
            place[c] = jnp.where(hit, rank[c] + (start - low), place[c])
            choice[c] = jnp.where(inside, b, choice[c])
            left[b][c] = left[b][c] - weight
            used[b][c] = low + weight
        start = start + weight
    down = lax.broadcasted_iota(jnp.int32, (size, size), 0)
    across = lax.broadcasted_iota(jnp.int32, (size, size), 1)
    code = choice[0]
    for c in range(1, groups):
        code = code + choice[c] * 4**c
    choice_ref[...] = code
    upright = [jnp.sum(jnp.where(down == across, place[c], 0), axis=1, keepdims=True) for c in range(groups)]
    store = pltpu.make_async_copy(second_buf, second_ref.at[0], sem)
    for channel, own_ref in ((1, second_buf), (0, first_ref)):
        for c in range(groups):
            order = one_hot(upright[c] == across)
            own = jnp.dot(table_ref[channel], order, preferred_element_type=jnp.float32)
            own_ref[c] = own.astype(jnp.bfloat16)
        if channel == 1:
            store.start()
    for b in range(groups):
        for at in range(0, size, 128):
            total = jnp.zeros((1, 128), jnp.int32)
            for c in range(groups):
                hit = lookup_ref[pl.ds(c * size, size)] == lane + (b * size + at)
                total += jnp.sum(jnp.where(hit, upright[c], 0), axis=0, keepdims=True)
            swap_ref[pl.ds(b, 1), pl.ds(at, 128)] = total
    store.wait()


def route(rows, lookup, table):
    groups, size = rows.shape
    _, twice, _ = table.shape
    return pl.pallas_call(
        route_kernel,
        out_shape=(
            jax.ShapeDtypeStruct((groups, size), jnp.int32),
            jax.ShapeDtypeStruct((size, 128), jnp.int32),
            jax.ShapeDtypeStruct((groups, twice, size), jnp.bfloat16),
            jax.ShapeDtypeStruct((12, groups, twice, size), jnp.bfloat16),
        ),
        in_specs=[pl.BlockSpec(memory_space=pltpu.VMEM)] * 3,
        out_specs=(pl.BlockSpec(memory_space=pltpu.VMEM),) * 3 + (pl.BlockSpec(memory_space=pl.ANY),),
        scratch_shapes=[pltpu.VMEM((groups, twice, size), jnp.bfloat16), pltpu.SemaphoreType.DMA],
        compiler_params=pltpu.CompilerParams(vmem_limit_bytes=44 * MEGA),
        cost_estimate=pl.CostEstimate(flops=2 * 2**30, bytes_accessed=8 * MEGA, transcendentals=0),
        name="route",
    )(rows, lookup, table)


def beams_kernel(turned_ref, swap_ref, choice_ref, first_ref, second_ref, out_ref, grid_ref, second_buf, sem):
    sources, channels, _, feeds, samples = turned_ref.shape
    feeds_total = sources * feeds
    cylinders, size = swap_ref.shape
    fetch = pltpu.make_async_copy(second_ref.at[0], second_buf, sem)
    fetch.start()
    down = lax.broadcasted_iota(jnp.int32, (size, size), 0)
    swap = [one_hot(swap_ref[b : b + 1] == down) for b in range(cylinders)]
    def swaps(channel):
        for part in range(2):
            own = turned_ref[:, channel, part].reshape(feeds_total, samples)
            moved = [
                jnp.dot(swap[b], own[b * size : b * size + size], preferred_element_type=jnp.float32)
                for b in range(cylinders)
            ]
            for at in range(0, samples, 128):
                for c in range(cylinders):
                    pick = (choice_ref[...] >> (2 * c)) & 3
                    got = moved[3][:, at : at + 128]
                    for b in range(3):
                        got = jnp.where(pick == b, moved[b][:, at : at + 128], got)
                    grid_ref[channel, c, part, :, pl.ds(at, 128)] = got.astype(jnp.bfloat16)

    def field_of(channel, table_ref, c):
        by_real, by_imag = [
            jnp.dot(table_ref[c], grid_ref[channel, c, part], preferred_element_type=jnp.float32)
            for part in range(2)
        ]
        return by_real[:size] + by_imag[size:], by_imag[:size] - by_real[size:]

    def powers(channel, field, rows):
        for row in rows:
            halves = []
            for at in range(0, samples, 128):
                re = [field[c][0][row : row + 8, at : at + 128] for c in range(cylinders)]
                im = [field[c][1][row : row + 8, at : at + 128] for c in range(cylinders)]
                halves.append(beam_powers(re, im))
            for e in range(cylinders):
                low = jnp.concatenate([halves[0][e][:4], halves[1][e][:4]], axis=0)
                high = jnp.concatenate([halves[0][e][4:], halves[1][e][4:]], axis=0)
                at = e * (size // 4) + row // 4
                out_ref[owner_slot(at), pl.ds(channel * 8, 8)] = low.astype(jnp.bfloat16)
                out_ref[owner_slot(at + 1), pl.ds(channel * 8, 8)] = high.astype(jnp.bfloat16)

    swaps(0)
    zero = [field_of(0, first_ref, c) for c in range(cylinders)]
    swaps(1)
    powers(0, zero, range(0, size // 2, 8))
    fetch.wait()
    one = []
    for c in range(cylinders):
        one.append(field_of(1, second_buf, c))
        powers(0, zero, range(size // 2 + c * size // 8, size // 2 + (c + 1) * size // 8, 8))
    powers(1, one, range(0, size, 8))


def form_beams(turned, swap, choice, first, second):
    sources, channels, _, feeds, samples = turned.shape
    feeds_total = sources * feeds
    return pl.pallas_call(
        beams_kernel,
        out_shape=jax.ShapeDtypeStruct((feeds_total // 4, 16, 128), jnp.bfloat16),
        in_specs=[pl.BlockSpec(memory_space=pltpu.VMEM)] * 4 + [pl.BlockSpec(memory_space=pl.ANY)],
        out_specs=pl.BlockSpec(memory_space=pltpu.VMEM),
        scratch_shapes=[
            pltpu.VMEM((channels, 4, 2, feeds_total // 4, samples), jnp.bfloat16),
            pltpu.VMEM(first.shape, jnp.bfloat16),
            pltpu.SemaphoreType.DMA,
        ],
        compiler_params=pltpu.CompilerParams(vmem_limit_bytes=44 * MEGA),
        cost_estimate=pl.CostEstimate(flops=3 * 2**29, bytes_accessed=8 * MEGA, transcendentals=0),
        name="form_beams",
    )(turned, swap, choice, first, second)


def total_kernel(sent_ref, out_ref, total_ref, out_buf, out_sem):
    chunks = out_sem.shape[0]
    block = total_ref.shape[0] // 16 // chunks

    def store(i):
        own = pl.ds(i * 2 * block, 2 * block)
        return pltpu.make_async_copy(out_buf.at[:, own], out_ref.at[:, own], out_sem.at[i])

    for i in range(chunks):
        for source in range(i * block, i * block + block):
            own = [sent_ref[owner_slot(source * 4 + stream)].astype(jnp.float32) for stream in range(4)]
            total_ref[pl.ds(source * 16, 16)] = (own[0] + own[1]) + (own[2] + own[3])
        for beam in range(4):
            for half in range(2):
                rows = total_ref[pl.ds(i * block * 16 + half * 4 + beam, 2 * block, stride=8)]
                out_buf[beam, pl.ds(i * 2 * block, 2 * block), pl.ds(half * 128, 128)] = rows
        store(i).start()
    for i in range(chunks):
        store(i).wait()


def add_streams(sent):
    blocks = sent.shape[0] // 4
    chunks = 4
    return pl.pallas_call(
        total_kernel,
        out_shape=jax.ShapeDtypeStruct((4, 2 * blocks, 256), jnp.float32),
        in_specs=[pl.BlockSpec(memory_space=pltpu.VMEM)],
        out_specs=pl.BlockSpec(memory_space=pl.ANY),
        scratch_shapes=[
            pltpu.VMEM((blocks * 16, 128), jnp.float32),
            pltpu.VMEM((4, 2 * blocks, 256), jnp.float32),
            pltpu.SemaphoreType.DMA((chunks,)),
        ],
        compiler_params=pltpu.CompilerParams(vmem_limit_bytes=16 * MEGA),
        cost_estimate=pl.CostEstimate(flops=2**20, bytes_accessed=2 * MEGA, transcendentals=0),
        name="add_streams",
    )(sent)


def body(voltages, gains, cylinder_feed_lookup, beam_bins):
    calibrated = calibrate(voltages, gains)
    turned = lax.all_to_all(calibrated, "wide", split_axis=0, concat_axis=0, tiled=True)
    lookup = jnp.broadcast_to(cylinder_feed_lookup[:, None], (cylinder_feed_lookup.shape[0], 128))
    table = dft_table(beam_bins, beam_bins.shape[1])
    swap, choice, first, second = route(cylinder_feed_lookup.reshape(4, -1), lookup, table)
    power = form_beams(turned, swap, choice, first, second)
    owners = power.shape[0]
    order = sorted(range(owners), key=owner_slot)
    sent = lax.all_to_all(
        power, ("wide", "pol"), split_axis=0, concat_axis=0, axis_index_groups=[order], tiled=True
    )
    return add_streams(sent)


def solution(mesh):
    return jax.shard_map(
        body,
        mesh=mesh,
        in_specs=(
            P(None, "pol", "wide", None, None),
            P(None, None, "wide", None),
            P(),
            P("wide", None),
        ),
        out_specs=P(("wide", "pol"), None, None),
        check_vma=False,
    )
```

```python
import itertools
import math

import jax
import jax.numpy as jnp
from jax import lax
from jax.experimental import pallas as pl
from jax.experimental.pallas import tpu as pltpu
from jax.sharding import PartitionSpec as P

MEGA = 2**20


def owner_slot(owner):
    x, y, z, core, stream = owner // 64, owner // 16 % 4, owner // 8 % 2, owner // 4 % 2, owner % 4
    return (stream * 2 + z) * 32 + (x * 4 + y) * 2 + core


def corner_slot(device):
    x, y, z, core = device // 16, device // 4 % 4, device // 2 % 2, device % 2
    return x * 16 + z * 8 + core * 4 + y


def dft_table(bins, feeds_per):
    along = lax.iota(jnp.int32, feeds_per)
    product = bins[:, :, None] * along[None, None, :] % (2 * feeds_per)
    theta = product.astype(jnp.float32) * (math.pi / feeds_per)
    cos_table = jnp.cos(theta).astype(jnp.bfloat16)
    sin_table = jnp.sin(theta).astype(jnp.bfloat16)
    return jnp.concatenate([cos_table, sin_table], axis=1)


def calibrate_kernel(volts_ref, gains_ref, out_ref, in_buf, gain_buf, out_buf, in_sem, gain_sem, out_sem):
    chunks, _, feeds, block, samples = in_buf.shape

    def fetch(i):
        own = volts_ref.at[:, 0, :, pl.ds(i * block, block), :]
        return pltpu.make_async_copy(own, in_buf.at[i], in_sem.at[i])

    def store(i):
        own = out_ref.at[pl.ds(i * block // 2, block // 2)]
        return pltpu.make_async_copy(out_buf.at[i], own, out_sem.at[i])

    gain_copy = pltpu.make_async_copy(gains_ref, gain_buf, gain_sem)
    gain_copy.start()
    for i in range(chunks):
        fetch(i).start()
    row = lax.broadcasted_iota(jnp.int32, (feeds * 16, feeds * 16), 0)
    col = lax.broadcasted_iota(jnp.int32, (feeds * 16, feeds * 16), 1)
    swap = (row // feeds == col % 16) & (row % feeds == col // 16)
    swap = swap.astype(jnp.float32).astype(jnp.bfloat16)
    gain_copy.wait()
    polar = lax.axis_index("pol") // 2
    gain_real = gain_buf[0, polar]
    gain_imag = gain_buf[1, polar]
    for i in range(chunks):
        fetch(i).wait()
        for group in range(block // 16):
            parts = []
            for part in range(2):
                own = in_buf[i, part, :, group * 16 : group * 16 + 16, :].reshape(feeds * 16, samples)
                parts.append(jnp.dot(swap, own, preferred_element_type=jnp.float32))
            for c in range(16):
                at = group * 16 + c
                channel = i * block + at
                own_real = gain_real[:, channel : channel + 1]
                own_imag = gain_imag[:, channel : channel + 1]
                volt_real = parts[0][c * feeds : c * feeds + feeds]
                volt_imag = parts[1][c * feeds : c * feeds + feeds]
                cal_real = own_real * volt_real - own_imag * volt_imag
                cal_imag = own_real * volt_imag + own_imag * volt_real
                out_buf[i, corner_slot(channel // 2) - i * block // 2, at % 2, 0] = cal_real.astype(jnp.bfloat16)
                out_buf[i, corner_slot(channel // 2) - i * block // 2, at % 2, 1] = cal_imag.astype(jnp.bfloat16)
        store(i).start()
    for i in range(chunks):
        store(i).wait()


def calibrate(voltages, gains):
    _, _, feeds, channels, samples = voltages.shape
    chunks = 2
    block = channels // chunks
    return pl.pallas_call(
        calibrate_kernel,
        out_shape=jax.ShapeDtypeStruct((channels // 2, 2, 2, feeds, samples), jnp.bfloat16),
        in_specs=[pl.BlockSpec(memory_space=pl.ANY)] * 2,
        out_specs=pl.BlockSpec(memory_space=pl.ANY),
        scratch_shapes=[
            pltpu.VMEM((chunks, 2, feeds, block, samples), jnp.bfloat16),
            pltpu.VMEM(gains.shape, jnp.float32),
            pltpu.VMEM((chunks, block // 2, 2, 2, feeds, samples), jnp.bfloat16),
            pltpu.SemaphoreType.DMA((chunks,)),
            pltpu.SemaphoreType.DMA,
            pltpu.SemaphoreType.DMA((chunks,)),
        ],
        compiler_params=pltpu.CompilerParams(vmem_limit_bytes=60 * MEGA),
        cost_estimate=pl.CostEstimate(flops=2**29, bytes_accessed=4 * MEGA, transcendentals=0),
        name="calibrate",
    )(voltages, gains)


def beam_powers(real_parts, imag_parts):
    sum_re, sum_im = real_parts[0] + real_parts[2], imag_parts[0] + imag_parts[2]
    dif_re, dif_im = real_parts[0] - real_parts[2], imag_parts[0] - imag_parts[2]
    odd_re, odd_im = real_parts[1] + real_parts[3], imag_parts[1] + imag_parts[3]
    odd_dif_re, odd_dif_im = real_parts[1] - real_parts[3], imag_parts[1] - imag_parts[3]
    each = [
        (sum_re + odd_re, sum_im + odd_im),
        (dif_re + odd_dif_im, dif_im - odd_dif_re),
        (sum_re - odd_re, sum_im - odd_im),
        (dif_re - odd_dif_im, dif_im + odd_dif_re),
    ]
    return [a * a + b * b for a, b in each]


def one_hot(hit):
    return hit.astype(jnp.float32).astype(jnp.bfloat16)


def route_kernel(rows_ref, lookup_ref, table_ref, swap_ref, choice_ref, first_ref, second_ref, second_buf, sem):
    groups, size = rows_ref.shape
    column = lax.broadcasted_iota(jnp.int32, (size, 128), 0)
    lane = lax.broadcasted_iota(jnp.int32, (size, 128), 1)
    block = [rows_ref[c : c + 1] >> 8 for c in range(groups)]
    rank, left = [], [[None] * groups for _ in range(groups)]
    for c in range(groups):
        own = lookup_ref[pl.ds(c * size, size)] >> 8
        parts = []
        for at in range(0, size, 128):
            before = (own == block[c][:, at : at + 128]) & (column < lane + at)
            parts.append(jnp.sum(before.astype(jnp.int32), axis=0, keepdims=True))
        rank.append(jnp.concatenate(parts, axis=1))
        for b in range(groups):
            left[b][c] = jnp.sum((block[c] == b).astype(jnp.int32))
    used = [[0] * groups for _ in range(groups)]
    place = [jnp.zeros((1, size), jnp.int32) for _ in range(groups)]
    choice = [jnp.zeros((size, 128), jnp.int32) for _ in range(groups)]
    start = 0
    for target in itertools.permutations(range(groups)):
        weight = left[0][target[0]]
        for b in range(1, groups):
            weight = jnp.minimum(weight, left[b][target[b]])
        inside = (column >= start) & (column < start + weight)
        for b in range(groups):
            c = target[b]
            low = used[b][c]
            hit = (block[c] == b) & (rank[c] >= low) & (rank[c] < low + weight)
            place[c] = jnp.where(hit, rank[c] + (start - low), place[c])
            choice[c] = jnp.where(inside, b, choice[c])
            left[b][c] = left[b][c] - weight
            used[b][c] = low + weight
        start = start + weight
    down = lax.broadcasted_iota(jnp.int32, (size, size), 0)
    across = lax.broadcasted_iota(jnp.int32, (size, size), 1)
    code = choice[0]
    for c in range(1, groups):
        code = code + choice[c] * 4**c
    choice_ref[...] = code
    upright = [jnp.sum(jnp.where(down == across, place[c], 0), axis=1, keepdims=True) for c in range(groups)]
    store = pltpu.make_async_copy(second_buf, second_ref.at[0], sem)
    for channel, own_ref in ((1, second_buf), (0, first_ref)):
        for c in range(groups):
            order = one_hot(upright[c] == across)
            own = jnp.dot(table_ref[channel], order, preferred_element_type=jnp.float32)
            own_ref[c] = own.astype(jnp.bfloat16)
        if channel == 1:
            store.start()
    for b in range(groups):
        for at in range(0, size, 128):
            total = jnp.zeros((1, 128), jnp.int32)
            for c in range(groups):
                hit = lookup_ref[pl.ds(c * size, size)] == lane + (b * size + at)
                total += jnp.sum(jnp.where(hit, upright[c], 0), axis=0, keepdims=True)
            swap_ref[pl.ds(b, 1), pl.ds(at, 128)] = total
    store.wait()


def route(rows, lookup, table):
    groups, size = rows.shape
    _, twice, _ = table.shape
    return pl.pallas_call(
        route_kernel,
        out_shape=(
            jax.ShapeDtypeStruct((groups, size), jnp.int32),
            jax.ShapeDtypeStruct((size, 128), jnp.int32),
            jax.ShapeDtypeStruct((groups, twice, size), jnp.bfloat16),
            jax.ShapeDtypeStruct((12, groups, twice, size), jnp.bfloat16),
        ),
        in_specs=[pl.BlockSpec(memory_space=pltpu.VMEM)] * 3,
        out_specs=(pl.BlockSpec(memory_space=pltpu.VMEM),) * 3 + (pl.BlockSpec(memory_space=pl.ANY),),
        scratch_shapes=[pltpu.VMEM((groups, twice, size), jnp.bfloat16), pltpu.SemaphoreType.DMA],
        compiler_params=pltpu.CompilerParams(vmem_limit_bytes=44 * MEGA),
        cost_estimate=pl.CostEstimate(flops=2 * 2**30, bytes_accessed=8 * MEGA, transcendentals=0),
        name="route",
    )(rows, lookup, table)


def beams_kernel(turned_ref, swap_ref, choice_ref, first_ref, second_ref, out_ref, grid_ref, second_buf, sem):
    sources, channels, _, feeds, samples = turned_ref.shape
    feeds_total = sources * feeds
    cylinders, size = swap_ref.shape
    fetch = pltpu.make_async_copy(second_ref.at[0], second_buf, sem)
    fetch.start()
    down = lax.broadcasted_iota(jnp.int32, (size, size), 0)
    swap = [one_hot(swap_ref[b : b + 1] == down) for b in range(cylinders)]
    def swaps(channel):
        for part in range(2):
            own = turned_ref[:, channel, part].reshape(feeds_total, samples)
            moved = [
                jnp.dot(swap[b], own[b * size : b * size + size], preferred_element_type=jnp.float32)
                for b in range(cylinders)
            ]
            for at in range(0, samples, 128):
                for c in range(cylinders):
                    pick = (choice_ref[...] >> (2 * c)) & 3
                    got = moved[3][:, at : at + 128]
                    for b in range(3):
                        got = jnp.where(pick == b, moved[b][:, at : at + 128], got)
                    grid_ref[channel, c, part, :, pl.ds(at, 128)] = got.astype(jnp.bfloat16)

    def field_of(channel, table_ref, c):
        by_real, by_imag = [
            jnp.dot(table_ref[c], grid_ref[channel, c, part], preferred_element_type=jnp.float32)
            for part in range(2)
        ]
        return by_real[:size] + by_imag[size:], by_imag[:size] - by_real[size:]

    def powers(channel, field, rows):
        for row in rows:
            halves = []
            for at in range(0, samples, 128):
                re = [field[c][0][row : row + 8, at : at + 128] for c in range(cylinders)]
                im = [field[c][1][row : row + 8, at : at + 128] for c in range(cylinders)]
                halves.append(beam_powers(re, im))
            for e in range(cylinders):
                low = jnp.concatenate([halves[0][e][:4], halves[1][e][:4]], axis=0)
                high = jnp.concatenate([halves[0][e][4:], halves[1][e][4:]], axis=0)
                at = e * (size // 4) + row // 4
                out_ref[owner_slot(at), pl.ds(channel * 8, 8)] = low.astype(jnp.bfloat16)
                out_ref[owner_slot(at + 1), pl.ds(channel * 8, 8)] = high.astype(jnp.bfloat16)

    swaps(0)
    zero = [field_of(0, first_ref, c) for c in range(cylinders)]
    swaps(1)
    powers(0, zero, range(0, size // 2, 8))
    fetch.wait()
    one = []
    for c in range(cylinders):
        one.append(field_of(1, second_buf, c))
        powers(0, zero, range(size // 2 + c * size // 8, size // 2 + (c + 1) * size // 8, 8))
    powers(1, one, range(0, size, 8))


def form_beams(turned, swap, choice, first, second):
    sources, channels, _, feeds, samples = turned.shape
    feeds_total = sources * feeds
    return pl.pallas_call(
        beams_kernel,
        out_shape=jax.ShapeDtypeStruct((feeds_total // 4, 16, 128), jnp.bfloat16),
        in_specs=[pl.BlockSpec(memory_space=pltpu.VMEM)] * 4 + [pl.BlockSpec(memory_space=pl.ANY)],
        out_specs=pl.BlockSpec(memory_space=pltpu.VMEM),
        scratch_shapes=[
            pltpu.VMEM((channels, 4, 2, feeds_total // 4, samples), jnp.bfloat16),
            pltpu.VMEM(first.shape, jnp.bfloat16),
            pltpu.SemaphoreType.DMA,
        ],
        compiler_params=pltpu.CompilerParams(vmem_limit_bytes=44 * MEGA),
        cost_estimate=pl.CostEstimate(flops=3 * 2**29, bytes_accessed=8 * MEGA, transcendentals=0),
        name="form_beams",
    )(turned, swap, choice, first, second)


def total_kernel(sent_ref, out_ref, total_ref, out_buf, out_sem):
    chunks = out_sem.shape[0]
    block = total_ref.shape[0] // 16 // chunks

    def store(i):
        own = pl.ds(i * 2 * block, 2 * block)
        return pltpu.make_async_copy(out_buf.at[:, own], out_ref.at[:, own], out_sem.at[i])

    for i in range(chunks):
        for source in range(i * block, i * block + block):
            own = [sent_ref[owner_slot(source * 4 + stream)].astype(jnp.float32) for stream in range(4)]
            total_ref[pl.ds(source * 16, 16)] = (own[0] + own[1]) + (own[2] + own[3])
        for beam in range(4):
            for half in range(2):
                rows = total_ref[pl.ds(i * block * 16 + half * 4 + beam, 2 * block, stride=8)]
                out_buf[beam, pl.ds(i * 2 * block, 2 * block), pl.ds(half * 128, 128)] = rows
        store(i).start()
    for i in range(chunks):
        store(i).wait()


def add_streams(sent):
    blocks = sent.shape[0] // 4
    chunks = 4
    return pl.pallas_call(
        total_kernel,
        out_shape=jax.ShapeDtypeStruct((4, 2 * blocks, 256), jnp.float32),
        in_specs=[pl.BlockSpec(memory_space=pltpu.VMEM)],
        out_specs=pl.BlockSpec(memory_space=pl.ANY),
        scratch_shapes=[
            pltpu.VMEM((blocks * 16, 128), jnp.float32),
            pltpu.VMEM((4, 2 * blocks, 256), jnp.float32),
            pltpu.SemaphoreType.DMA((chunks,)),
        ],
        compiler_params=pltpu.CompilerParams(vmem_limit_bytes=16 * MEGA),
        cost_estimate=pl.CostEstimate(flops=2**20, bytes_accessed=2 * MEGA, transcendentals=0),
        name="add_streams",
    )(sent)


def body(voltages, gains, cylinder_feed_lookup, beam_bins):
    calibrated = calibrate(voltages, gains)
    devices = calibrated.shape[0]
    order = sorted(range(devices), key=corner_slot)
    turned = lax.all_to_all(
        calibrated, "wide", split_axis=0, concat_axis=0, axis_index_groups=[order], tiled=True
    )
    cylinder_feed_lookup = corner_slot(cylinder_feed_lookup // 16) * 16 + cylinder_feed_lookup % 16
    lookup = jnp.broadcast_to(cylinder_feed_lookup[:, None], (cylinder_feed_lookup.shape[0], 128))
    table = dft_table(beam_bins, beam_bins.shape[1])
    swap, choice, first, second = route(cylinder_feed_lookup.reshape(4, -1), lookup, table)
    power = form_beams(turned, swap, choice, first, second)
    owners = power.shape[0]
    order = sorted(range(owners), key=owner_slot)
    sent = lax.all_to_all(
        power, ("wide", "pol"), split_axis=0, concat_axis=0, axis_index_groups=[order], tiled=True
    )
    return add_streams(sent)


def solution(mesh):
    return jax.shard_map(
        body,
        mesh=mesh,
        in_specs=(
            P(None, "pol", "wide", None, None),
            P(None, None, "wide", None),
            P(),
            P("wide", None),
        ),
        out_specs=P(("wide", "pol"), None, None),
        check_vma=False,
    )
```

```python
import itertools
import math

import jax
import jax.numpy as jnp
from jax import lax
from jax.experimental import pallas as pl
from jax.experimental.pallas import tpu as pltpu
from jax.sharding import PartitionSpec as P

MEGA = 2**20


def owner_slot(owner):
    x, y, z, core, stream = owner // 64, owner // 16 % 4, owner // 8 % 2, owner // 4 % 2, owner % 4
    return (stream * 2 + z) * 32 + (x * 4 + y) * 2 + core


def corner_slot(device):
    x, y, z, core = device // 16, device // 4 % 4, device // 2 % 2, device % 2
    return x * 16 + core * 8 + z * 4 + y


def dft_table(bins, feeds_per):
    along = lax.iota(jnp.int32, feeds_per)
    product = bins[:, :, None] * along[None, None, :] % (2 * feeds_per)
    theta = product.astype(jnp.float32) * (math.pi / feeds_per)
    cos_table = jnp.cos(theta).astype(jnp.bfloat16)
    sin_table = jnp.sin(theta).astype(jnp.bfloat16)
    return jnp.concatenate([cos_table, sin_table], axis=1)


def calibrate_kernel(volts_ref, gains_ref, out_ref, in_buf, gain_buf, out_buf, in_sem, gain_sem, out_sem):
    chunks, _, feeds, block, samples = in_buf.shape

    def fetch(i):
        own = volts_ref.at[:, 0, :, pl.ds(i * block, block), :]
        return pltpu.make_async_copy(own, in_buf.at[i], in_sem.at[i])

    def store(i):
        own = out_ref.at[pl.ds(i * block // 2, block // 2)]
        return pltpu.make_async_copy(out_buf.at[i], own, out_sem.at[i])

    gain_copy = pltpu.make_async_copy(gains_ref, gain_buf, gain_sem)
    gain_copy.start()
    for i in range(chunks):
        fetch(i).start()
    row = lax.broadcasted_iota(jnp.int32, (feeds * 16, feeds * 16), 0)
    col = lax.broadcasted_iota(jnp.int32, (feeds * 16, feeds * 16), 1)
    swap = (row // feeds == col % 16) & (row % feeds == col // 16)
    swap = swap.astype(jnp.float32).astype(jnp.bfloat16)
    gain_copy.wait()
    polar = lax.axis_index("pol") // 2
    gain_real = gain_buf[0, polar]
    gain_imag = gain_buf[1, polar]
    for i in range(chunks):
        fetch(i).wait()
        for group in range(block // 16):
            parts = []
            for part in range(2):
                own = in_buf[i, part, :, group * 16 : group * 16 + 16, :].reshape(feeds * 16, samples)
                parts.append(jnp.dot(swap, own, preferred_element_type=jnp.float32))
            for c in range(16):
                at = group * 16 + c
                channel = i * block + at
                own_real = gain_real[:, channel : channel + 1]
                own_imag = gain_imag[:, channel : channel + 1]
                volt_real = parts[0][c * feeds : c * feeds + feeds]
                volt_imag = parts[1][c * feeds : c * feeds + feeds]
                cal_real = own_real * volt_real - own_imag * volt_imag
                cal_imag = own_real * volt_imag + own_imag * volt_real
                out_buf[i, corner_slot(channel // 2) - i * block // 2, at % 2, 0] = cal_real.astype(jnp.bfloat16)
                out_buf[i, corner_slot(channel // 2) - i * block // 2, at % 2, 1] = cal_imag.astype(jnp.bfloat16)
        store(i).start()
    for i in range(chunks):
        store(i).wait()


def calibrate(voltages, gains):
    _, _, feeds, channels, samples = voltages.shape
    chunks = 2
    block = channels // chunks
    return pl.pallas_call(
        calibrate_kernel,
        out_shape=jax.ShapeDtypeStruct((channels // 2, 2, 2, feeds, samples), jnp.bfloat16),
        in_specs=[pl.BlockSpec(memory_space=pl.ANY)] * 2,
        out_specs=pl.BlockSpec(memory_space=pl.ANY),
        scratch_shapes=[
            pltpu.VMEM((chunks, 2, feeds, block, samples), jnp.bfloat16),
            pltpu.VMEM(gains.shape, jnp.float32),
            pltpu.VMEM((chunks, block // 2, 2, 2, feeds, samples), jnp.bfloat16),
            pltpu.SemaphoreType.DMA((chunks,)),
            pltpu.SemaphoreType.DMA,
            pltpu.SemaphoreType.DMA((chunks,)),
        ],
        compiler_params=pltpu.CompilerParams(vmem_limit_bytes=60 * MEGA),
        cost_estimate=pl.CostEstimate(flops=2**29, bytes_accessed=4 * MEGA, transcendentals=0),
        name="calibrate",
    )(voltages, gains)


def beam_powers(real_parts, imag_parts):
    sum_re, sum_im = real_parts[0] + real_parts[2], imag_parts[0] + imag_parts[2]
    dif_re, dif_im = real_parts[0] - real_parts[2], imag_parts[0] - imag_parts[2]
    odd_re, odd_im = real_parts[1] + real_parts[3], imag_parts[1] + imag_parts[3]
    odd_dif_re, odd_dif_im = real_parts[1] - real_parts[3], imag_parts[1] - imag_parts[3]
    each = [
        (sum_re + odd_re, sum_im + odd_im),
        (dif_re + odd_dif_im, dif_im - odd_dif_re),
        (sum_re - odd_re, sum_im - odd_im),
        (dif_re - odd_dif_im, dif_im + odd_dif_re),
    ]
    return [a * a + b * b for a, b in each]


def one_hot(hit):
    return hit.astype(jnp.float32).astype(jnp.bfloat16)


def route_kernel(rows_ref, lookup_ref, table_ref, swap_ref, choice_ref, first_ref, second_ref, second_buf, sem):
    groups, size = rows_ref.shape
    column = lax.broadcasted_iota(jnp.int32, (size, 128), 0)
    lane = lax.broadcasted_iota(jnp.int32, (size, 128), 1)
    block = [rows_ref[c : c + 1] >> 8 for c in range(groups)]
    rank, left = [], [[None] * groups for _ in range(groups)]
    for c in range(groups):
        own = lookup_ref[pl.ds(c * size, size)] >> 8
        parts = []
        for at in range(0, size, 128):
            before = (own == block[c][:, at : at + 128]) & (column < lane + at)
            parts.append(jnp.sum(before.astype(jnp.int32), axis=0, keepdims=True))
        rank.append(jnp.concatenate(parts, axis=1))
        for b in range(groups):
            left[b][c] = jnp.sum((block[c] == b).astype(jnp.int32))
    used = [[0] * groups for _ in range(groups)]
    place = [jnp.zeros((1, size), jnp.int32) for _ in range(groups)]
    choice = [jnp.zeros((size, 128), jnp.int32) for _ in range(groups)]
    start = 0
    for target in itertools.permutations(range(groups)):
        weight = left[0][target[0]]
        for b in range(1, groups):
            weight = jnp.minimum(weight, left[b][target[b]])
        inside = (column >= start) & (column < start + weight)
        for b in range(groups):
            c = target[b]
            low = used[b][c]
            hit = (block[c] == b) & (rank[c] >= low) & (rank[c] < low + weight)
            place[c] = jnp.where(hit, rank[c] + (start - low), place[c])
            choice[c] = jnp.where(inside, b, choice[c])
            left[b][c] = left[b][c] - weight
            used[b][c] = low + weight
        start = start + weight
    down = lax.broadcasted_iota(jnp.int32, (size, size), 0)
    across = lax.broadcasted_iota(jnp.int32, (size, size), 1)
    code = choice[0]
    for c in range(1, groups):
        code = code + choice[c] * 4**c
    choice_ref[...] = code
    upright = [jnp.sum(jnp.where(down == across, place[c], 0), axis=1, keepdims=True) for c in range(groups)]
    store = pltpu.make_async_copy(second_buf, second_ref.at[0], sem)
    for channel, own_ref in ((1, second_buf), (0, first_ref)):
        for c in range(groups):
            order = one_hot(upright[c] == across)
            own = jnp.dot(table_ref[channel], order, preferred_element_type=jnp.float32)
            own_ref[c] = own.astype(jnp.bfloat16)
        if channel == 1:
            store.start()
    for b in range(groups):
        for at in range(0, size, 128):
            total = jnp.zeros((1, 128), jnp.int32)
            for c in range(groups):
                hit = lookup_ref[pl.ds(c * size, size)] == lane + (b * size + at)
                total += jnp.sum(jnp.where(hit, upright[c], 0), axis=0, keepdims=True)
            swap_ref[pl.ds(b, 1), pl.ds(at, 128)] = total
    store.wait()


def route(rows, lookup, table):
    groups, size = rows.shape
    _, twice, _ = table.shape
    return pl.pallas_call(
        route_kernel,
        out_shape=(
            jax.ShapeDtypeStruct((groups, size), jnp.int32),
            jax.ShapeDtypeStruct((size, 128), jnp.int32),
            jax.ShapeDtypeStruct((groups, twice, size), jnp.bfloat16),
            jax.ShapeDtypeStruct((12, groups, twice, size), jnp.bfloat16),
        ),
        in_specs=[pl.BlockSpec(memory_space=pltpu.VMEM)] * 3,
        out_specs=(pl.BlockSpec(memory_space=pltpu.VMEM),) * 3 + (pl.BlockSpec(memory_space=pl.ANY),),
        scratch_shapes=[pltpu.VMEM((groups, twice, size), jnp.bfloat16), pltpu.SemaphoreType.DMA],
        compiler_params=pltpu.CompilerParams(vmem_limit_bytes=44 * MEGA),
        cost_estimate=pl.CostEstimate(flops=2 * 2**30, bytes_accessed=8 * MEGA, transcendentals=0),
        name="route",
    )(rows, lookup, table)


def beams_kernel(turned_ref, swap_ref, choice_ref, first_ref, second_ref, out_ref, grid_ref, second_buf, sem):
    sources, channels, _, feeds, samples = turned_ref.shape
    feeds_total = sources * feeds
    cylinders, size = swap_ref.shape
    fetch = pltpu.make_async_copy(second_ref.at[0], second_buf, sem)
    fetch.start()
    down = lax.broadcasted_iota(jnp.int32, (size, size), 0)
    swap = [one_hot(swap_ref[b : b + 1] == down) for b in range(cylinders)]
    def swaps(channel):
        for part in range(2):
            own = turned_ref[:, channel, part].reshape(feeds_total, samples)
            moved = [
                jnp.dot(swap[b], own[b * size : b * size + size], preferred_element_type=jnp.float32)
                for b in range(cylinders)
            ]
            for at in range(0, samples, 128):
                for c in range(cylinders):
                    pick = (choice_ref[...] >> (2 * c)) & 3
                    got = moved[3][:, at : at + 128]
                    for b in range(3):
                        got = jnp.where(pick == b, moved[b][:, at : at + 128], got)
                    grid_ref[channel, c, part, :, pl.ds(at, 128)] = got.astype(jnp.bfloat16)

    def field_of(channel, table_ref, c):
        by_real, by_imag = [
            jnp.dot(table_ref[c], grid_ref[channel, c, part], preferred_element_type=jnp.float32)
            for part in range(2)
        ]
        return by_real[:size] + by_imag[size:], by_imag[:size] - by_real[size:]

    def powers(channel, field, rows):
        for row in rows:
            halves = []
            for at in range(0, samples, 128):
                re = [field[c][0][row : row + 8, at : at + 128] for c in range(cylinders)]
                im = [field[c][1][row : row + 8, at : at + 128] for c in range(cylinders)]
                halves.append(beam_powers(re, im))
            for e in range(cylinders):
                low = jnp.concatenate([halves[0][e][:4], halves[1][e][:4]], axis=0)
                high = jnp.concatenate([halves[0][e][4:], halves[1][e][4:]], axis=0)
                at = e * (size // 4) + row // 4
                out_ref[owner_slot(at), pl.ds(channel * 8, 8)] = low.astype(jnp.bfloat16)
                out_ref[owner_slot(at + 1), pl.ds(channel * 8, 8)] = high.astype(jnp.bfloat16)

    swaps(0)
    zero = [field_of(0, first_ref, c) for c in range(cylinders)]
    swaps(1)
    powers(0, zero, range(0, size // 2, 8))
    fetch.wait()
    one = []
    for c in range(cylinders):
        one.append(field_of(1, second_buf, c))
        powers(0, zero, range(size // 2 + c * size // 8, size // 2 + (c + 1) * size // 8, 8))
    powers(1, one, range(0, size, 8))


def form_beams(turned, swap, choice, first, second):
    sources, channels, _, feeds, samples = turned.shape
    feeds_total = sources * feeds
    return pl.pallas_call(
        beams_kernel,
        out_shape=jax.ShapeDtypeStruct((feeds_total // 4, 16, 128), jnp.bfloat16),
        in_specs=[pl.BlockSpec(memory_space=pltpu.VMEM)] * 4 + [pl.BlockSpec(memory_space=pl.ANY)],
        out_specs=pl.BlockSpec(memory_space=pltpu.VMEM),
        scratch_shapes=[
            pltpu.VMEM((channels, 4, 2, feeds_total // 4, samples), jnp.bfloat16),
            pltpu.VMEM(first.shape, jnp.bfloat16),
            pltpu.SemaphoreType.DMA,
        ],
        compiler_params=pltpu.CompilerParams(vmem_limit_bytes=44 * MEGA),
        cost_estimate=pl.CostEstimate(flops=3 * 2**29, bytes_accessed=8 * MEGA, transcendentals=0),
        name="form_beams",
    )(turned, swap, choice, first, second)


def total_kernel(sent_ref, out_ref, total_ref, out_buf, out_sem):
    chunks = out_sem.shape[0]
    block = total_ref.shape[0] // 16 // chunks

    def store(i):
        own = pl.ds(i * 2 * block, 2 * block)
        return pltpu.make_async_copy(out_buf.at[:, own], out_ref.at[:, own], out_sem.at[i])

    for i in range(chunks):
        for source in range(i * block, i * block + block):
            own = [sent_ref[owner_slot(source * 4 + stream)].astype(jnp.float32) for stream in range(4)]
            total_ref[pl.ds(source * 16, 16)] = (own[0] + own[1]) + (own[2] + own[3])
        for beam in range(4):
            for half in range(2):
                rows = total_ref[pl.ds(i * block * 16 + half * 4 + beam, 2 * block, stride=8)]
                out_buf[beam, pl.ds(i * 2 * block, 2 * block), pl.ds(half * 128, 128)] = rows
        store(i).start()
    for i in range(chunks):
        store(i).wait()


def add_streams(sent):
    blocks = sent.shape[0] // 4
    chunks = 4
    return pl.pallas_call(
        total_kernel,
        out_shape=jax.ShapeDtypeStruct((4, 2 * blocks, 256), jnp.float32),
        in_specs=[pl.BlockSpec(memory_space=pltpu.VMEM)],
        out_specs=pl.BlockSpec(memory_space=pl.ANY),
        scratch_shapes=[
            pltpu.VMEM((blocks * 16, 128), jnp.float32),
            pltpu.VMEM((4, 2 * blocks, 256), jnp.float32),
            pltpu.SemaphoreType.DMA((chunks,)),
        ],
        compiler_params=pltpu.CompilerParams(vmem_limit_bytes=16 * MEGA),
        cost_estimate=pl.CostEstimate(flops=2**20, bytes_accessed=2 * MEGA, transcendentals=0),
        name="add_streams",
    )(sent)


def body(voltages, gains, cylinder_feed_lookup, beam_bins):
    calibrated = calibrate(voltages, gains)
    devices = calibrated.shape[0]
    order = sorted(range(devices), key=corner_slot)
    turned = lax.all_to_all(
        calibrated, "wide", split_axis=0, concat_axis=0, axis_index_groups=[order], tiled=True
    )
    cylinder_feed_lookup = corner_slot(cylinder_feed_lookup // 16) * 16 + cylinder_feed_lookup % 16
    lookup = jnp.broadcast_to(cylinder_feed_lookup[:, None], (cylinder_feed_lookup.shape[0], 128))
    table = dft_table(beam_bins, beam_bins.shape[1])
    swap, choice, first, second = route(cylinder_feed_lookup.reshape(4, -1), lookup, table)
    power = form_beams(turned, swap, choice, first, second)
    owners = power.shape[0]
    order = sorted(range(owners), key=owner_slot)
    sent = lax.all_to_all(
        power, ("wide", "pol"), split_axis=0, concat_axis=0, axis_index_groups=[order], tiled=True
    )
    return add_streams(sent)


def solution(mesh):
    return jax.shard_map(
        body,
        mesh=mesh,
        in_specs=(
            P(None, "pol", "wide", None, None),
            P(None, None, "wide", None),
            P(),
            P("wide", None),
        ),
        out_specs=P(("wide", "pol"), None, None),
        check_vma=False,
    )
```

```python
import itertools
import math

import jax
import jax.numpy as jnp
from jax import lax
from jax.experimental import pallas as pl
from jax.experimental.pallas import tpu as pltpu
from jax.sharding import PartitionSpec as P

MEGA = 2**20


def owner_slot(owner):
    x, y, z, core, stream = owner // 64, owner // 16 % 4, owner // 8 % 2, owner // 4 % 2, owner % 4
    return (stream * 2 + z) * 32 + (x * 4 + y) * 2 + core


def corner_slot(device):
    x, y, z, core = device // 16, device // 4 % 4, device // 2 % 2, device % 2
    return x * 16 + core * 8 + z * 4 + 3 - y


def dft_table(bins, feeds_per):
    along = lax.iota(jnp.int32, feeds_per)
    product = bins[:, :, None] * along[None, None, :] % (2 * feeds_per)
    theta = product.astype(jnp.float32) * (math.pi / feeds_per)
    cos_table = jnp.cos(theta).astype(jnp.bfloat16)
    sin_table = jnp.sin(theta).astype(jnp.bfloat16)
    return jnp.concatenate([cos_table, sin_table], axis=1)


def calibrate_kernel(volts_ref, gains_ref, out_ref, in_buf, gain_buf, out_buf, in_sem, gain_sem, out_sem):
    chunks, _, feeds, block, samples = in_buf.shape

    def fetch(i):
        own = volts_ref.at[:, 0, :, pl.ds(i * block, block), :]
        return pltpu.make_async_copy(own, in_buf.at[i], in_sem.at[i])

    def store(i):
        own = out_ref.at[pl.ds(i * block // 2, block // 2)]
        return pltpu.make_async_copy(out_buf.at[i], own, out_sem.at[i])

    gain_copy = pltpu.make_async_copy(gains_ref, gain_buf, gain_sem)
    gain_copy.start()
    for i in range(chunks):
        fetch(i).start()
    row = lax.broadcasted_iota(jnp.int32, (feeds * 16, feeds * 16), 0)
    col = lax.broadcasted_iota(jnp.int32, (feeds * 16, feeds * 16), 1)
    swap = (row // feeds == col % 16) & (row % feeds == col // 16)
    swap = swap.astype(jnp.float32).astype(jnp.bfloat16)
    gain_copy.wait()
    polar = lax.axis_index("pol") // 2
    gain_real = gain_buf[0, polar]
    gain_imag = gain_buf[1, polar]
    for i in range(chunks):
        fetch(i).wait()
        for group in range(block // 16):
            parts = []
            for part in range(2):
                own = in_buf[i, part, :, group * 16 : group * 16 + 16, :].reshape(feeds * 16, samples)
                parts.append(jnp.dot(swap, own, preferred_element_type=jnp.float32))
            for c in range(16):
                at = group * 16 + c
                channel = i * block + at
                own_real = gain_real[:, channel : channel + 1]
                own_imag = gain_imag[:, channel : channel + 1]
                volt_real = parts[0][c * feeds : c * feeds + feeds]
                volt_imag = parts[1][c * feeds : c * feeds + feeds]
                cal_real = own_real * volt_real - own_imag * volt_imag
                cal_imag = own_real * volt_imag + own_imag * volt_real
                out_buf[i, corner_slot(channel // 2) - i * block // 2, at % 2, 0] = cal_real.astype(jnp.bfloat16)
                out_buf[i, corner_slot(channel // 2) - i * block // 2, at % 2, 1] = cal_imag.astype(jnp.bfloat16)
        store(i).start()
    for i in range(chunks):
        store(i).wait()


def calibrate(voltages, gains):
    _, _, feeds, channels, samples = voltages.shape
    chunks = 2
    block = channels // chunks
    return pl.pallas_call(
        calibrate_kernel,
        out_shape=jax.ShapeDtypeStruct((channels // 2, 2, 2, feeds, samples), jnp.bfloat16),
        in_specs=[pl.BlockSpec(memory_space=pl.ANY)] * 2,
        out_specs=pl.BlockSpec(memory_space=pl.ANY),
        scratch_shapes=[
            pltpu.VMEM((chunks, 2, feeds, block, samples), jnp.bfloat16),
            pltpu.VMEM(gains.shape, jnp.float32),
            pltpu.VMEM((chunks, block // 2, 2, 2, feeds, samples), jnp.bfloat16),
            pltpu.SemaphoreType.DMA((chunks,)),
            pltpu.SemaphoreType.DMA,
            pltpu.SemaphoreType.DMA((chunks,)),
        ],
        compiler_params=pltpu.CompilerParams(vmem_limit_bytes=60 * MEGA),
        cost_estimate=pl.CostEstimate(flops=2**29, bytes_accessed=4 * MEGA, transcendentals=0),
        name="calibrate",
    )(voltages, gains)


def beam_powers(real_parts, imag_parts):
    sum_re, sum_im = real_parts[0] + real_parts[2], imag_parts[0] + imag_parts[2]
    dif_re, dif_im = real_parts[0] - real_parts[2], imag_parts[0] - imag_parts[2]
    odd_re, odd_im = real_parts[1] + real_parts[3], imag_parts[1] + imag_parts[3]
    odd_dif_re, odd_dif_im = real_parts[1] - real_parts[3], imag_parts[1] - imag_parts[3]
    each = [
        (sum_re + odd_re, sum_im + odd_im),
        (dif_re + odd_dif_im, dif_im - odd_dif_re),
        (sum_re - odd_re, sum_im - odd_im),
        (dif_re - odd_dif_im, dif_im + odd_dif_re),
    ]
    return [a * a + b * b for a, b in each]


def one_hot(hit):
    return hit.astype(jnp.float32).astype(jnp.bfloat16)


def route_kernel(rows_ref, lookup_ref, table_ref, swap_ref, choice_ref, first_ref, second_ref, second_buf, sem):
    groups, size = rows_ref.shape
    column = lax.broadcasted_iota(jnp.int32, (size, 128), 0)
    lane = lax.broadcasted_iota(jnp.int32, (size, 128), 1)
    block = [rows_ref[c : c + 1] >> 8 for c in range(groups)]
    rank, left = [], [[None] * groups for _ in range(groups)]
    for c in range(groups):
        own = lookup_ref[pl.ds(c * size, size)] >> 8
        parts = []
        for at in range(0, size, 128):
            before = (own == block[c][:, at : at + 128]) & (column < lane + at)
            parts.append(jnp.sum(before.astype(jnp.int32), axis=0, keepdims=True))
        rank.append(jnp.concatenate(parts, axis=1))
        for b in range(groups):
            left[b][c] = jnp.sum((block[c] == b).astype(jnp.int32))
    used = [[0] * groups for _ in range(groups)]
    place = [jnp.zeros((1, size), jnp.int32) for _ in range(groups)]
    choice = [jnp.zeros((size, 128), jnp.int32) for _ in range(groups)]
    start = 0
    for target in itertools.permutations(range(groups)):
        weight = left[0][target[0]]
        for b in range(1, groups):
            weight = jnp.minimum(weight, left[b][target[b]])
        inside = (column >= start) & (column < start + weight)
        for b in range(groups):
            c = target[b]
            low = used[b][c]
            hit = (block[c] == b) & (rank[c] >= low) & (rank[c] < low + weight)
            place[c] = jnp.where(hit, rank[c] + (start - low), place[c])
            choice[c] = jnp.where(inside, b, choice[c])
            left[b][c] = left[b][c] - weight
            used[b][c] = low + weight
        start = start + weight
    down = lax.broadcasted_iota(jnp.int32, (size, size), 0)
    across = lax.broadcasted_iota(jnp.int32, (size, size), 1)
    code = choice[0]
    for c in range(1, groups):
        code = code + choice[c] * 4**c
    choice_ref[...] = code
    upright = [jnp.sum(jnp.where(down == across, place[c], 0), axis=1, keepdims=True) for c in range(groups)]
    store = pltpu.make_async_copy(second_buf, second_ref.at[0], sem)
    for channel, own_ref in ((1, second_buf), (0, first_ref)):
        for c in range(groups):
            order = one_hot(upright[c] == across)
            own = jnp.dot(table_ref[channel], order, preferred_element_type=jnp.float32)
            own_ref[c] = own.astype(jnp.bfloat16)
        if channel == 1:
            store.start()
    for b in range(groups):
        for at in range(0, size, 128):
            total = jnp.zeros((1, 128), jnp.int32)
            for c in range(groups):
                hit = lookup_ref[pl.ds(c * size, size)] == lane + (b * size + at)
                total += jnp.sum(jnp.where(hit, upright[c], 0), axis=0, keepdims=True)
            swap_ref[pl.ds(b, 1), pl.ds(at, 128)] = total
    store.wait()


def route(rows, lookup, table):
    groups, size = rows.shape
    _, twice, _ = table.shape
    return pl.pallas_call(
        route_kernel,
        out_shape=(
            jax.ShapeDtypeStruct((groups, size), jnp.int32),
            jax.ShapeDtypeStruct((size, 128), jnp.int32),
            jax.ShapeDtypeStruct((groups, twice, size), jnp.bfloat16),
            jax.ShapeDtypeStruct((12, groups, twice, size), jnp.bfloat16),
        ),
        in_specs=[pl.BlockSpec(memory_space=pltpu.VMEM)] * 3,
        out_specs=(pl.BlockSpec(memory_space=pltpu.VMEM),) * 3 + (pl.BlockSpec(memory_space=pl.ANY),),
        scratch_shapes=[pltpu.VMEM((groups, twice, size), jnp.bfloat16), pltpu.SemaphoreType.DMA],
        compiler_params=pltpu.CompilerParams(vmem_limit_bytes=44 * MEGA),
        cost_estimate=pl.CostEstimate(flops=2 * 2**30, bytes_accessed=8 * MEGA, transcendentals=0),
        name="route",
    )(rows, lookup, table)


def beams_kernel(turned_ref, swap_ref, choice_ref, first_ref, second_ref, out_ref, grid_ref, second_buf, sem):
    sources, channels, _, feeds, samples = turned_ref.shape
    feeds_total = sources * feeds
    cylinders, size = swap_ref.shape
    fetch = pltpu.make_async_copy(second_ref.at[0], second_buf, sem)
    fetch.start()
    down = lax.broadcasted_iota(jnp.int32, (size, size), 0)
    swap = [one_hot(swap_ref[b : b + 1] == down) for b in range(cylinders)]
    def swaps(channel):
        for part in range(2):
            own = turned_ref[:, channel, part].reshape(feeds_total, samples)
            moved = [
                jnp.dot(swap[b], own[b * size : b * size + size], preferred_element_type=jnp.float32)
                for b in range(cylinders)
            ]
            for at in range(0, samples, 128):
                for c in range(cylinders):
                    pick = (choice_ref[...] >> (2 * c)) & 3
                    got = moved[3][:, at : at + 128]
                    for b in range(3):
                        got = jnp.where(pick == b, moved[b][:, at : at + 128], got)
                    grid_ref[channel, c, part, :, pl.ds(at, 128)] = got.astype(jnp.bfloat16)

    def field_of(channel, table_ref, c):
        by_real, by_imag = [
            jnp.dot(table_ref[c], grid_ref[channel, c, part], preferred_element_type=jnp.float32)
            for part in range(2)
        ]
        return by_real[:size] + by_imag[size:], by_imag[:size] - by_real[size:]

    def powers(channel, field, rows):
        for row in rows:
            halves = []
            for at in range(0, samples, 128):
                re = [field[c][0][row : row + 8, at : at + 128] for c in range(cylinders)]
                im = [field[c][1][row : row + 8, at : at + 128] for c in range(cylinders)]
                halves.append(beam_powers(re, im))
            for e in range(cylinders):
                low = jnp.concatenate([halves[0][e][:4], halves[1][e][:4]], axis=0)
                high = jnp.concatenate([halves[0][e][4:], halves[1][e][4:]], axis=0)
                at = e * (size // 4) + row // 4
                out_ref[owner_slot(at), pl.ds(channel * 8, 8)] = low.astype(jnp.bfloat16)
                out_ref[owner_slot(at + 1), pl.ds(channel * 8, 8)] = high.astype(jnp.bfloat16)

    swaps(0)
    zero = [field_of(0, first_ref, c) for c in range(cylinders)]
    swaps(1)
    powers(0, zero, range(0, size // 2, 8))
    fetch.wait()
    one = []
    for c in range(cylinders):
        one.append(field_of(1, second_buf, c))
        powers(0, zero, range(size // 2 + c * size // 8, size // 2 + (c + 1) * size // 8, 8))
    powers(1, one, range(0, size, 8))


def form_beams(turned, swap, choice, first, second):
    sources, channels, _, feeds, samples = turned.shape
    feeds_total = sources * feeds
    return pl.pallas_call(
        beams_kernel,
        out_shape=jax.ShapeDtypeStruct((feeds_total // 4, 16, 128), jnp.bfloat16),
        in_specs=[pl.BlockSpec(memory_space=pltpu.VMEM)] * 4 + [pl.BlockSpec(memory_space=pl.ANY)],
        out_specs=pl.BlockSpec(memory_space=pltpu.VMEM),
        scratch_shapes=[
            pltpu.VMEM((channels, 4, 2, feeds_total // 4, samples), jnp.bfloat16),
            pltpu.VMEM(first.shape, jnp.bfloat16),
            pltpu.SemaphoreType.DMA,
        ],
        compiler_params=pltpu.CompilerParams(vmem_limit_bytes=44 * MEGA),
        cost_estimate=pl.CostEstimate(flops=3 * 2**29, bytes_accessed=8 * MEGA, transcendentals=0),
        name="form_beams",
    )(turned, swap, choice, first, second)


def total_kernel(sent_ref, out_ref, total_ref, out_buf, out_sem):
    chunks = out_sem.shape[0]
    block = total_ref.shape[0] // 16 // chunks

    def store(i):
        own = pl.ds(i * 2 * block, 2 * block)
        return pltpu.make_async_copy(out_buf.at[:, own], out_ref.at[:, own], out_sem.at[i])

    for i in range(chunks):
        for source in range(i * block, i * block + block):
            own = [sent_ref[owner_slot(source * 4 + stream)].astype(jnp.float32) for stream in range(4)]
            total_ref[pl.ds(source * 16, 16)] = (own[0] + own[1]) + (own[2] + own[3])
        for beam in range(4):
            for half in range(2):
                rows = total_ref[pl.ds(i * block * 16 + half * 4 + beam, 2 * block, stride=8)]
                out_buf[beam, pl.ds(i * 2 * block, 2 * block), pl.ds(half * 128, 128)] = rows
        store(i).start()
    for i in range(chunks):
        store(i).wait()


def add_streams(sent):
    blocks = sent.shape[0] // 4
    chunks = 4
    return pl.pallas_call(
        total_kernel,
        out_shape=jax.ShapeDtypeStruct((4, 2 * blocks, 256), jnp.float32),
        in_specs=[pl.BlockSpec(memory_space=pltpu.VMEM)],
        out_specs=pl.BlockSpec(memory_space=pl.ANY),
        scratch_shapes=[
            pltpu.VMEM((blocks * 16, 128), jnp.float32),
            pltpu.VMEM((4, 2 * blocks, 256), jnp.float32),
            pltpu.SemaphoreType.DMA((chunks,)),
        ],
        compiler_params=pltpu.CompilerParams(vmem_limit_bytes=16 * MEGA),
        cost_estimate=pl.CostEstimate(flops=2**20, bytes_accessed=2 * MEGA, transcendentals=0),
        name="add_streams",
    )(sent)


def body(voltages, gains, cylinder_feed_lookup, beam_bins):
    calibrated = calibrate(voltages, gains)
    devices = calibrated.shape[0]
    order = sorted(range(devices), key=corner_slot)
    turned = lax.all_to_all(
        calibrated, "wide", split_axis=0, concat_axis=0, axis_index_groups=[order], tiled=True
    )
    cylinder_feed_lookup = corner_slot(cylinder_feed_lookup // 16) * 16 + cylinder_feed_lookup % 16
    lookup = jnp.broadcast_to(cylinder_feed_lookup[:, None], (cylinder_feed_lookup.shape[0], 128))
    table = dft_table(beam_bins, beam_bins.shape[1])
    swap, choice, first, second = route(cylinder_feed_lookup.reshape(4, -1), lookup, table)
    power = form_beams(turned, swap, choice, first, second)
    owners = power.shape[0]
    order = sorted(range(owners), key=owner_slot)
    sent = lax.all_to_all(
        power, ("wide", "pol"), split_axis=0, concat_axis=0, axis_index_groups=[order], tiled=True
    )
    return add_streams(sent)


def solution(mesh):
    return jax.shard_map(
        body,
        mesh=mesh,
        in_specs=(
            P(None, "pol", "wide", None, None),
            P(None, None, "wide", None),
            P(),
            P("wide", None),
        ),
        out_specs=P(("wide", "pol"), None, None),
        check_vma=False,
    )
```

```python
import itertools
import math

import jax
import jax.numpy as jnp
from jax import lax
from jax.experimental import pallas as pl
from jax.experimental.pallas import tpu as pltpu
from jax.sharding import PartitionSpec as P

MEGA = 2**20


def owner_slot(owner):
    x, y, z, core, stream = owner // 64, owner // 16 % 4, owner // 8 % 2, owner // 4 % 2, owner % 4
    return (stream * 2 + z) * 32 + (x * 4 + y) * 2 + core


def corner_slot(device):
    x, y, z, core = device // 16, device // 4 % 4, device // 2 % 2, device % 2
    return x * 16 + core * 8 + z * 4 + y


def dft_table(bins, feeds_per):
    along = lax.iota(jnp.int32, feeds_per)
    product = bins[:, :, None] * along[None, None, :] % (2 * feeds_per)
    theta = product.astype(jnp.float32) * (math.pi / feeds_per)
    cos_table = jnp.cos(theta).astype(jnp.bfloat16)
    sin_table = jnp.sin(theta).astype(jnp.bfloat16)
    return jnp.concatenate([cos_table, sin_table], axis=1)


def calibrate_kernel(volts_ref, gains_ref, out_ref, in_buf, gain_buf, out_buf, in_sem, gain_sem, out_sem):
    chunks, _, feeds, block, samples = in_buf.shape

    def fetch(i):
        own = volts_ref.at[:, 0, :, pl.ds(i * block, block), :]
        return pltpu.make_async_copy(own, in_buf.at[i], in_sem.at[i])

    def store(i):
        own = out_ref.at[pl.ds(i * block // 2, block // 2)]
        return pltpu.make_async_copy(out_buf.at[i], own, out_sem.at[i])

    gain_copy = pltpu.make_async_copy(gains_ref, gain_buf, gain_sem)
    gain_copy.start()
    for i in range(chunks):
        fetch(i).start()
    row = lax.broadcasted_iota(jnp.int32, (feeds * 16, feeds * 16), 0)
    col = lax.broadcasted_iota(jnp.int32, (feeds * 16, feeds * 16), 1)
    swap = (row // feeds == col % 16) & (row % feeds == col // 16)
    swap = swap.astype(jnp.float32).astype(jnp.bfloat16)
    gain_copy.wait()
    polar = lax.axis_index("pol") // 2
    gain_real = gain_buf[0, polar]
    gain_imag = gain_buf[1, polar]
    for i in range(chunks):
        fetch(i).wait()
        for group in range(block // 16):
            parts = []
            for part in range(2):
                own = in_buf[i, part, :, group * 16 : group * 16 + 16, :].reshape(feeds * 16, samples)
                parts.append(jnp.dot(swap, own, preferred_element_type=jnp.float32))
            for c in range(16):
                at = group * 16 + c
                channel = i * block + at
                own_real = gain_real[:, channel : channel + 1]
                own_imag = gain_imag[:, channel : channel + 1]
                volt_real = parts[0][c * feeds : c * feeds + feeds]
                volt_imag = parts[1][c * feeds : c * feeds + feeds]
                cal_real = own_real * volt_real - own_imag * volt_imag
                cal_imag = own_real * volt_imag + own_imag * volt_real
                out_buf[i, corner_slot(channel // 2) - i * block // 2, at % 2, 0] = cal_real.astype(jnp.bfloat16)
                out_buf[i, corner_slot(channel // 2) - i * block // 2, at % 2, 1] = cal_imag.astype(jnp.bfloat16)
        store(i).start()
    for i in range(chunks):
        store(i).wait()


def calibrate(voltages, gains):
    _, _, feeds, channels, samples = voltages.shape
    chunks = 2
    block = channels // chunks
    return pl.pallas_call(
        calibrate_kernel,
        out_shape=jax.ShapeDtypeStruct((channels // 2, 2, 2, feeds, samples), jnp.bfloat16),
        in_specs=[pl.BlockSpec(memory_space=pl.ANY)] * 2,
        out_specs=pl.BlockSpec(memory_space=pl.ANY),
        scratch_shapes=[
            pltpu.VMEM((chunks, 2, feeds, block, samples), jnp.bfloat16),
            pltpu.VMEM(gains.shape, jnp.float32),
            pltpu.VMEM((chunks, block // 2, 2, 2, feeds, samples), jnp.bfloat16),
            pltpu.SemaphoreType.DMA((chunks,)),
            pltpu.SemaphoreType.DMA,
            pltpu.SemaphoreType.DMA((chunks,)),
        ],
        compiler_params=pltpu.CompilerParams(vmem_limit_bytes=60 * MEGA),
        cost_estimate=pl.CostEstimate(flops=2**29, bytes_accessed=4 * MEGA, transcendentals=0),
        name="calibrate",
    )(voltages, gains)


def beam_powers(real_parts, imag_parts):
    sum_re, sum_im = real_parts[0] + real_parts[2], imag_parts[0] + imag_parts[2]
    dif_re, dif_im = real_parts[0] - real_parts[2], imag_parts[0] - imag_parts[2]
    odd_re, odd_im = real_parts[1] + real_parts[3], imag_parts[1] + imag_parts[3]
    odd_dif_re, odd_dif_im = real_parts[1] - real_parts[3], imag_parts[1] - imag_parts[3]
    each = [
        (sum_re + odd_re, sum_im + odd_im),
        (dif_re + odd_dif_im, dif_im - odd_dif_re),
        (sum_re - odd_re, sum_im - odd_im),
        (dif_re - odd_dif_im, dif_im + odd_dif_re),
    ]
    return [a * a + b * b for a, b in each]


def one_hot(hit):
    return hit.astype(jnp.float32).astype(jnp.bfloat16)


def route_kernel(rows_ref, lookup_ref, table_ref, swap_ref, choice_ref, first_ref, second_ref, second_buf, sem):
    groups, size = rows_ref.shape
    column = lax.broadcasted_iota(jnp.int32, (size, 128), 0)
    lane = lax.broadcasted_iota(jnp.int32, (size, 128), 1)
    block = [rows_ref[c : c + 1] >> 8 for c in range(groups)]
    rank, left = [], [[None] * groups for _ in range(groups)]
    for c in range(groups):
        own = lookup_ref[pl.ds(c * size, size)] >> 8
        parts = []
        for at in range(0, size, 128):
            before = (own == block[c][:, at : at + 128]) & (column < lane + at)
            parts.append(jnp.sum(before.astype(jnp.int32), axis=0, keepdims=True))
        rank.append(jnp.concatenate(parts, axis=1))
        for b in range(groups):
            left[b][c] = jnp.sum((block[c] == b).astype(jnp.int32))
    used = [[0] * groups for _ in range(groups)]
    place = [jnp.zeros((1, size), jnp.int32) for _ in range(groups)]
    choice = [jnp.zeros((size, 128), jnp.int32) for _ in range(groups)]
    start = 0
    for target in itertools.permutations(range(groups)):
        weight = left[0][target[0]]
        for b in range(1, groups):
            weight = jnp.minimum(weight, left[b][target[b]])
        inside = (column >= start) & (column < start + weight)
        for b in range(groups):
            c = target[b]
            low = used[b][c]
            hit = (block[c] == b) & (rank[c] >= low) & (rank[c] < low + weight)
            place[c] = jnp.where(hit, rank[c] + (start - low), place[c])
            choice[c] = jnp.where(inside, b, choice[c])
            left[b][c] = left[b][c] - weight
            used[b][c] = low + weight
        start = start + weight
    down = lax.broadcasted_iota(jnp.int32, (size, size), 0)
    across = lax.broadcasted_iota(jnp.int32, (size, size), 1)
    code = choice[0]
    for c in range(1, groups):
        code = code + choice[c] * 4**c
    choice_ref[...] = code
    upright = [jnp.sum(jnp.where(down == across, place[c], 0), axis=1, keepdims=True) for c in range(groups)]
    store = pltpu.make_async_copy(second_buf, second_ref.at[0], sem)
    for channel, own_ref in ((1, second_buf), (0, first_ref)):
        for c in range(groups):
            order = one_hot(upright[c] == across)
            own = jnp.dot(table_ref[channel], order, preferred_element_type=jnp.float32)
            own_ref[c] = own.astype(jnp.bfloat16)
        if channel == 1:
            store.start()
    for b in range(groups):
        for at in range(0, size, 128):
            total = jnp.zeros((1, 128), jnp.int32)
            for c in range(groups):
                hit = lookup_ref[pl.ds(c * size, size)] == lane + (b * size + at)
                total += jnp.sum(jnp.where(hit, upright[c], 0), axis=0, keepdims=True)
            swap_ref[pl.ds(b, 1), pl.ds(at, 128)] = total
    store.wait()


def route(rows, lookup, table):
    groups, size = rows.shape
    _, twice, _ = table.shape
    return pl.pallas_call(
        route_kernel,
        out_shape=(
            jax.ShapeDtypeStruct((groups, size), jnp.int32),
            jax.ShapeDtypeStruct((size, 128), jnp.int32),
            jax.ShapeDtypeStruct((groups, twice, size), jnp.bfloat16),
            jax.ShapeDtypeStruct((12, groups, twice, size), jnp.bfloat16),
        ),
        in_specs=[pl.BlockSpec(memory_space=pltpu.VMEM)] * 3,
        out_specs=(pl.BlockSpec(memory_space=pltpu.VMEM),) * 3 + (pl.BlockSpec(memory_space=pl.ANY),),
        scratch_shapes=[pltpu.VMEM((groups, twice, size), jnp.bfloat16), pltpu.SemaphoreType.DMA],
        compiler_params=pltpu.CompilerParams(vmem_limit_bytes=44 * MEGA),
        cost_estimate=pl.CostEstimate(flops=2 * 2**30, bytes_accessed=8 * MEGA, transcendentals=0),
        name="route",
    )(rows, lookup, table)


def beams_kernel(turned_ref, swap_ref, choice_ref, first_ref, second_ref, out_ref, grid_ref, second_buf, sem):
    sources, channels, _, feeds, samples = turned_ref.shape
    feeds_total = sources * feeds
    cylinders, size = swap_ref.shape
    fetch = pltpu.make_async_copy(second_ref.at[0], second_buf, sem)
    fetch.start()
    down = lax.broadcasted_iota(jnp.int32, (size, size), 0)
    swap = [one_hot(swap_ref[b : b + 1] == down) for b in range(cylinders)]
    def swaps(channel):
        for part in range(2):
            own = turned_ref[:, channel, part].reshape(feeds_total, samples)
            moved = [
                jnp.dot(swap[b], own[b * size : b * size + size], preferred_element_type=jnp.float32)
                for b in range(cylinders)
            ]
            for at in range(0, samples, 128):
                for c in range(cylinders):
                    pick = (choice_ref[...] >> (2 * c)) & 3
                    got = moved[3][:, at : at + 128]
                    for b in range(3):
                        got = jnp.where(pick == b, moved[b][:, at : at + 128], got)
                    grid_ref[channel, c, part, :, pl.ds(at, 128)] = got.astype(jnp.bfloat16)

    def field_of(channel, table_ref, c):
        by_real, by_imag = [
            jnp.dot(table_ref[c], grid_ref[channel, c, part], preferred_element_type=jnp.float32)
            for part in range(2)
        ]
        return by_real[:size] + by_imag[size:], by_imag[:size] - by_real[size:]

    def powers(channel, field, rows):
        for row in rows:
            halves = []
            for at in range(0, samples, 128):
                re = [field[c][0][row : row + 8, at : at + 128] for c in range(cylinders)]
                im = [field[c][1][row : row + 8, at : at + 128] for c in range(cylinders)]
                halves.append(beam_powers(re, im))
            for e in range(cylinders):
                low = jnp.concatenate([halves[0][e][:4], halves[1][e][:4]], axis=0)
                high = jnp.concatenate([halves[0][e][4:], halves[1][e][4:]], axis=0)
                at = e * (size // 4) + row // 4
                out_ref[owner_slot(at), pl.ds(channel * 8, 8)] = low.astype(jnp.bfloat16)
                out_ref[owner_slot(at + 1), pl.ds(channel * 8, 8)] = high.astype(jnp.bfloat16)

    swaps(0)
    zero = [field_of(0, first_ref, c) for c in range(cylinders)]
    swaps(1)
    fetch.wait()
    one = [field_of(1, second_buf, c) for c in range(cylinders)]
    powers(0, zero, range(0, size, 8))
    powers(1, one, range(0, size, 8))


def form_beams(turned, swap, choice, first, second):
    sources, channels, _, feeds, samples = turned.shape
    feeds_total = sources * feeds
    return pl.pallas_call(
        beams_kernel,
        out_shape=jax.ShapeDtypeStruct((feeds_total // 4, 16, 128), jnp.bfloat16),
        in_specs=[pl.BlockSpec(memory_space=pltpu.VMEM)] * 4 + [pl.BlockSpec(memory_space=pl.ANY)],
        out_specs=pl.BlockSpec(memory_space=pltpu.VMEM),
        scratch_shapes=[
            pltpu.VMEM((channels, 4, 2, feeds_total // 4, samples), jnp.bfloat16),
            pltpu.VMEM(first.shape, jnp.bfloat16),
            pltpu.SemaphoreType.DMA,
        ],
        compiler_params=pltpu.CompilerParams(vmem_limit_bytes=44 * MEGA),
        cost_estimate=pl.CostEstimate(flops=3 * 2**29, bytes_accessed=8 * MEGA, transcendentals=0),
        name="form_beams",
    )(turned, swap, choice, first, second)


def total_kernel(sent_ref, out_ref, total_ref, out_buf, out_sem):
    chunks = out_sem.shape[0]
    block = total_ref.shape[0] // 16 // chunks

    def store(i):
        own = pl.ds(i * 2 * block, 2 * block)
        return pltpu.make_async_copy(out_buf.at[:, own], out_ref.at[:, own], out_sem.at[i])

    for i in range(chunks):
        for source in range(i * block, i * block + block):
            own = [sent_ref[owner_slot(source * 4 + stream)].astype(jnp.float32) for stream in range(4)]
            total_ref[pl.ds(source * 16, 16)] = (own[0] + own[1]) + (own[2] + own[3])
        for beam in range(4):
            for half in range(2):
                rows = total_ref[pl.ds(i * block * 16 + half * 4 + beam, 2 * block, stride=8)]
                out_buf[beam, pl.ds(i * 2 * block, 2 * block), pl.ds(half * 128, 128)] = rows
        store(i).start()
    for i in range(chunks):
        store(i).wait()


def add_streams(sent):
    blocks = sent.shape[0] // 4
    chunks = 4
    return pl.pallas_call(
        total_kernel,
        out_shape=jax.ShapeDtypeStruct((4, 2 * blocks, 256), jnp.float32),
        in_specs=[pl.BlockSpec(memory_space=pltpu.VMEM)],
        out_specs=pl.BlockSpec(memory_space=pl.ANY),
        scratch_shapes=[
            pltpu.VMEM((blocks * 16, 128), jnp.float32),
            pltpu.VMEM((4, 2 * blocks, 256), jnp.float32),
            pltpu.SemaphoreType.DMA((chunks,)),
        ],
        compiler_params=pltpu.CompilerParams(vmem_limit_bytes=16 * MEGA),
        cost_estimate=pl.CostEstimate(flops=2**20, bytes_accessed=2 * MEGA, transcendentals=0),
        name="add_streams",
    )(sent)


def body(voltages, gains, cylinder_feed_lookup, beam_bins):
    calibrated = calibrate(voltages, gains)
    devices = calibrated.shape[0]
    order = sorted(range(devices), key=corner_slot)
    turned = lax.all_to_all(
        calibrated, "wide", split_axis=0, concat_axis=0, axis_index_groups=[order], tiled=True
    )
    cylinder_feed_lookup = corner_slot(cylinder_feed_lookup // 16) * 16 + cylinder_feed_lookup % 16
    lookup = jnp.broadcast_to(cylinder_feed_lookup[:, None], (cylinder_feed_lookup.shape[0], 128))
    table = dft_table(beam_bins, beam_bins.shape[1])
    swap, choice, first, second = route(cylinder_feed_lookup.reshape(4, -1), lookup, table)
    power = form_beams(turned, swap, choice, first, second)
    owners = power.shape[0]
    order = sorted(range(owners), key=owner_slot)
    sent = lax.all_to_all(
        power, ("wide", "pol"), split_axis=0, concat_axis=0, axis_index_groups=[order], tiled=True
    )
    return add_streams(sent)


def solution(mesh):
    return jax.shard_map(
        body,
        mesh=mesh,
        in_specs=(
            P(None, "pol", "wide", None, None),
            P(None, None, "wide", None),
            P(),
            P("wide", None),
        ),
        out_specs=P(("wide", "pol"), None, None),
        check_vma=False,
    )
```
